256 devices in a mesh: dom: 128 (over z, x, y), mp: 2 (over core).
Axes of the slice: x: 4, y: 4, z: 8, core: 2. Of those that a mesh axis runs over, the one named last changes fastest.
Arguments:
- tokens: bfloat16 [106496, 768], P('dom'), may hold values from -16 to 16
- up_weight: bfloat16 [768, 3072], P(None, 'mp'), may hold values from -0.21875 to 0.21875
- down_weight: bfloat16 [3072, 768], P('mp'), may hold values from -0.109375 to 0.109375
- text_owner: int32 [13312, 1], replicated, may hold values from 0 to 127; in each aligned block of 104 rows (0 to 103, 104 to 207, ...) at most 2 rows name the same one
- text_row: int32 [13312], replicated, may hold values from 0 to 255
- node_feat: bfloat16 [32768, 768], P('dom', 'mp'), may hold values from -6 to 6
- local_weight: bfloat16 [32768, 256], P('dom'), may hold values from 0 to 1
- tile_weight: bfloat16 [32768, 4, 128], P('dom'), may hold values from 0 to 1
- tile_peer: int32 [128, 4], P('dom'), may hold values from 0 to 3
- boundary_rows: int32 [128, 128], P('dom'), may hold values from 0 to 255
- self_weight: bfloat16 [2, 768, 768], P(None, None, 'mp'), may hold values from -0.21875 to 0.21875
- neigh_weight: bfloat16 [2, 768, 768], P(None, None, 'mp'), may hold values from -0.4375 to 0.4375
- node_cot: bfloat16 [32768, 768], P('dom', 'mp'), may hold values from -6 to 6
Outputs:
- node_out: bfloat16 [32768, 768], P('dom', 'mp')
- text_grad: float32 [13312, 768], P('dom', 'mp')
- down_grad: float32 [768, 3072], P('dom', 'mp')
The draws below stay inside these ranges and needn't reach their ends.
Inputs may be any that keep to these rules, and one draw needn't show every extreme that they name: `text_owner`: in the 104 texts of one shard (aligned blocks of rows), no owner is named more than 2 times, and in every draw some owner is named exactly 2 times.
All inputs are finite; a program needn't handle non-finite values.
Results may differ from the reference program's by a relative error of at most 0.018.
Values may be sent and summed in bfloat16 or wider, within the bound.
A program may use at most 128 MiB of HBM per device.

```python
import math
import jax
import jax.numpy as jnp
import numpy as np
from jax import lax

D = 768
FF = 3072
TXT_DEV = 104
SEQ = 8
NODE_DEV = 256
BND = 128
TILES = 4
SPAN = 4
LAYERS = 2
CAP = 2
PARTITIONS = 128
TEXTS = 13312
TOKENS = 106496
NODES = 32768


def sparse_weights(key, shape, density, power):
    value_key, mask_key = jax.random.split(key)
    magnitude = 0.1 + 0.9 * jax.random.uniform(value_key, shape, jnp.float32) ** power
    present = jax.random.uniform(mask_key, shape, jnp.float32) < density
    return jnp.where(present, magnitude, 0.0)


def draw_local_weight(key, part):
    key = jax.random.fold_in(key, 21)
    power = 1.0
    return sparse_weights(key, (NODES, NODE_DEV), 1.0 / 32.0, power).astype(jnp.bfloat16)


def draw_tile_weight(key, part):
    key = jax.random.fold_in(key, 22)
    power = 1.0
    return sparse_weights(key, (NODES, TILES, BND), 1.0 / 16.0, power).astype(jnp.bfloat16)


def draw_tokens(key, part):
    key = jax.random.fold_in(key, 23)
    keys = jax.random.split(key, 4)
    low = math.log(0.4)
    high = math.log(2.5)
    column_scale = jnp.exp(jax.random.uniform(keys[0], (1, 1, D), jnp.float32, low, high))
    row_scale = jnp.exp(jax.random.uniform(keys[1], (TEXTS, 1, 1), jnp.float32, low, high))
    shared = jax.random.normal(keys[2], (TEXTS, 1, D), jnp.float32)
    noise = jax.random.normal(keys[3], (TEXTS, SEQ, D), jnp.float32)
    values = row_scale * column_scale * (0.6 * shared + 0.8 * noise)
    return jnp.clip(values, -16.0, 16.0).reshape(TOKENS, D).astype(jnp.bfloat16)


def with_ends(result, stream_key, least, high):
    longest = result.shape.index(max(result.shape))
    spots = []
    for shift in (0, 1):
        where = [jax.random.randint(jax.random.fold_in(stream_key, axis), (), 0, length) for axis, length in enumerate(result.shape)]
        where[longest] = (where[longest] + shift) % result.shape[longest]
        spots.append(tuple(where))
    return result.at[spots[0]].set(least).at[spots[1]].set(high)


def steps_of(key, shape, shards, least, top_value):
    def one(axis_at, shards_of):
        heights = jax.random.uniform(jax.random.fold_in(jax.random.fold_in(key, 6), axis_at), (shards_of,), jnp.float32, least / len(shards), top_value / len(shards))
        return jnp.repeat(jnp.exp(heights), shape[axis_at] // shards_of).reshape((-1,) + (1,) * (len(shape) - axis_at - 1))

    gain = one(*shards[0])
    for cut in shards[1:]:
        gain = gain * one(*cut)
    return gain


def deal_out(own_key, own, number, rows, amount, top, most, slope):
    ranking = jax.random.permutation(own_key, amount)
    crowded, ordinary = shares(amount, rows * top, most, slope, True), shares(amount, rows * top, most, slope, False)
    places = jnp.arange(amount)

    def named(lengths, turn):
        used = int((lengths > 0).sum())
        fixed = max(1, used // 4)
        passed = fixed + (places - fixed + turn * (used - fixed)) % max(1, amount - fixed)
        return jnp.zeros((amount,), jnp.int32).at[ranking[jnp.where(places < fixed, places, passed)]].set(jnp.asarray(lengths, jnp.int32))

    lengths = jnp.where(number % 4 == 0, named(crowded, number // 4), named(ordinary, number - number // 4 - 1))
    mixed = jax.random.permutation(jax.random.fold_in(own, 3), amount)
    source_of, sink = mixed[0:amount // 2 * 2:2], mixed[1:amount // 2 * 2:2]
    room = jnp.minimum(lengths[source_of] - 1, most - lengths[sink]) // 2
    room = jnp.where((source_of == ranking[0]) | (sink == ranking[0]) | (lengths[sink] == 0), 0, jnp.maximum(room, 0))
    passed = jax.random.randint(jax.random.fold_in(own, 4), (amount // 2,), 0, 1 << 20) % (room + 1)
    lengths = lengths.at[source_of].add(-passed).at[sink].add(passed)
    labels = jnp.searchsorted(jnp.cumsum(lengths), jnp.arange(rows * top), side="right").astype(jnp.int32)
    table = labels.reshape(top, rows).T
    table = table[jax.random.permutation(jax.random.fold_in(own, 1), rows)]
    turn = jax.random.randint(jax.random.fold_in(own, 2), (rows, 1), 0, top)
    return jnp.take_along_axis(table, (jnp.arange(top)[None, :] + turn) % top, axis=1)


def shares(count, total, bound, slope, full):
    portions = [(1 << 20) // math.isqrt(standing ** slope) + 1 for standing in range(1, count + 1)]
    largest = bound if full else min(bound, max(-(-total // count), total * portions[0] // sum(portions)))
    least = 1 if total - largest >= count - 1 else 0
    given, surplus = [largest] + [least] * (count - 1), total - largest - least * (count - 1)
    while surplus > 0:
        free = [i for i in range(1, count) if given[i] < largest] or [i for i in range(1, count) if given[i] < bound]
        whole, left = sum([portions[i] for i in free]), surplus
        for i in free:
            extra = min(bound - given[i], max(1, left * portions[i] // whole), surplus)
            given[i] = given[i] + extra
            surplus = surplus - extra
    return np.array(given)


def scatter_about(key, extent, spread, limit, cuts=(), held_as=jnp.bfloat16):
    loudness = steps_of(key, extent, cuts, -0.22, 0.18) if cuts else 1.0
    result = jax.random.normal(key, extent, jnp.float32) * spread * loudness
    return jnp.minimum(jnp.maximum(result, -limit), limit).astype(held_as)


def setup_inputs(seed: int = 0) -> dict:
    key_list = jax.random.split(jax.random.key(seed), 14)
    tokens = draw_tokens(jax.random.fold_in(key_list[13], 71), 0)
    up_weight = scatter_about(key_list[1], (D, FF), D ** -0.5, 0.21875, ((1, 2),))
    down_weight = scatter_about(key_list[2], (FF, D), FF ** -0.5, 0.109375, ((0, 2),))
    text_owner_keys = jax.random.split(jax.random.fold_in(key_list[3], 1), TEXTS // TXT_DEV)
    text_owner_turns = jax.random.permutation(jax.random.fold_in(key_list[3], 3), TEXTS // TXT_DEV)
    text_owner = jax.vmap(lambda own, number: deal_out(jax.random.fold_in(key_list[3], 2), own, number, TXT_DEV, PARTITIONS, 1, CAP, 2))(text_owner_keys, text_owner_turns).reshape((TEXTS, 1))
    text_row = with_ends(jax.random.randint(key_list[4], (TEXTS,), 0, NODE_DEV), jax.random.fold_in(key_list[4], 1), 0, NODE_DEV - 1).astype(jnp.int32)
    node_feat = scatter_about(key_list[5], (NODES, D), 1.0, 6.0, ((0, 128), (1, 2)))
    local_weight = draw_local_weight(jax.random.fold_in(key_list[13], 71), 0)
    tile_weight = draw_tile_weight(jax.random.fold_in(key_list[13], 71), 0)
    tile_peer = with_ends(jax.random.randint(key_list[8], (PARTITIONS, TILES), 0, SPAN), jax.random.fold_in(key_list[8], 1), 0, SPAN - 1).astype(jnp.int32)
    boundary_rows = with_ends(jax.random.randint(key_list[9], (PARTITIONS, BND), 0, NODE_DEV), jax.random.fold_in(key_list[9], 1), 0, NODE_DEV - 1).astype(jnp.int32)
    self_weight = scatter_about(key_list[10], (LAYERS, D, D), D ** -0.5, 0.21875, ((2, 2),))
    neigh_weight = scatter_about(key_list[11], (LAYERS, D, D), (D // 4) ** -0.5, 0.4375, ((2, 2),))
    node_cot = scatter_about(key_list[12], (NODES, D), 1.0, 6.0, ((0, 128), (1, 2)))
    return dict(tokens=tokens, up_weight=up_weight, down_weight=down_weight, text_owner=text_owner, text_row=text_row, node_feat=node_feat, local_weight=local_weight, tile_weight=tile_weight, tile_peer=tile_peer, boundary_rows=boundary_rows, self_weight=self_weight, neigh_weight=neigh_weight, node_cot=node_cot)


def exact_gelu(inputs):
    return jax.nn.gelu(inputs, approximate=False)

def lead_contract(left, right):
    return lax.dot_general(left, right, (((0,), (0,)), ((), ())), preferred_element_type=jnp.float32)

def reference(tokens, up_weight, down_weight, text_owner, text_row, node_feat, local_weight, tile_weight, tile_peer, boundary_rows, self_weight, neigh_weight, node_cot):
    blocks = tokens.reshape(TEXTS, SEQ, D)

    def pool_one(block):
        hidden = exact_gelu(jnp.dot(block, up_weight, preferred_element_type=jnp.float32))
        return (lax.optimization_barrier(jnp.mean(hidden, axis=0)).astype(jnp.bfloat16), lax.optimization_barrier(jnp.mean(block.astype(jnp.float32), axis=0)))
    text_hidden, token_mean = lax.map(pool_one, blocks)
    pooled = token_mean + jnp.dot(text_hidden, down_weight, preferred_element_type=jnp.float32)
    centre = pooled - lax.optimization_barrier(jnp.mean(pooled, axis=-1, keepdims=True))
    inv_std = lax.rsqrt(lax.optimization_barrier(jnp.mean(centre * centre, axis=-1, keepdims=True)) + 1e-05)
    normed = centre * inv_std
    emb = normed.astype(jnp.bfloat16)
    target = (text_owner[:, 0] * NODE_DEV + text_row).astype(jnp.int32)
    start_rows = node_feat.astype(jnp.float32).at[target].add(emb.astype(jnp.float32))
    node_state = start_rows.astype(jnp.bfloat16)
    near_dev = local_weight.reshape(PARTITIONS, NODE_DEV, NODE_DEV)
    tiles_dev = tile_weight.reshape(PARTITIONS, NODE_DEV, TILES * BND)
    degree = 1.0 + lax.optimization_barrier(jnp.sum(local_weight.astype(jnp.float32), axis=1)) + lax.optimization_barrier(jnp.sum(tile_weight.astype(jnp.float32), axis=(1, 2)))
    degree_dev = degree.reshape(PARTITIONS, NODE_DEV)
    sources = jnp.mod(jnp.arange(PARTITIONS, dtype=jnp.int32)[:, None] - 1 - tile_peer, PARTITIONS).astype(jnp.int32)
    part_index = jnp.arange(PARTITIONS, dtype=jnp.int32)

    def aggregate(rows_all):
        rows_dev = rows_all.reshape(PARTITIONS, NODE_DEV, D)
        border = rows_dev[part_index[:, None], boundary_rows]

        def one_part(pieces):
            rows_here, near_here, tiles_here, src_here, degree_here = pieces
            remote = border[src_here].reshape(TILES * BND, D)
            total_sum = rows_here.astype(jnp.float32) + jnp.dot(near_here, rows_here, preferred_element_type=jnp.float32)
            total_sum = total_sum + jnp.dot(tiles_here, remote, preferred_element_type=jnp.float32)
            return (total_sum / degree_here[:, None]).astype(jnp.bfloat16)
        return lax.map(one_part, (rows_dev, near_dev, tiles_dev, sources, degree_dev)).reshape(NODES, D)
    pre_acts = []
    for layer_index in range(LAYERS):
        means = aggregate(node_state)
        pre_act = jnp.dot(node_state, self_weight[layer_index], preferred_element_type=jnp.float32)
        pre_act = pre_act + jnp.dot(means, neigh_weight[layer_index], preferred_element_type=jnp.float32)
        pre_acts.append(pre_act)
        node_state = exact_gelu(pre_act).astype(jnp.bfloat16)
    node_out = node_state
    node_grad = node_cot.astype(jnp.float32)
    for layer_index in reversed(range(LAYERS)):
        _, pull_back = jax.vjp(exact_gelu, pre_acts[layer_index])
        grad_pre = pull_back(node_grad)[0].astype(jnp.bfloat16)
        self_part = jnp.dot(grad_pre, self_weight[layer_index].T, preferred_element_type=jnp.float32)
        mean_part = jnp.dot(grad_pre, neigh_weight[layer_index].T, preferred_element_type=jnp.float32)
        scaled = (mean_part / degree[:, None]).astype(jnp.bfloat16)
        scaled_dev = scaled.reshape(PARTITIONS, NODE_DEV, D)

        def back_one(pieces):
            scaled_here, near_here, tiles_here = pieces
            local_sum = scaled_here.astype(jnp.float32) + lead_contract(near_here, scaled_here)
            sent = lead_contract(tiles_here, scaled_here)
            return (local_sum, sent.reshape(TILES, BND, D))
        local_sum, sent = lax.map(back_one, (scaled_dev, near_dev, tiles_dev))
        arrived = jax.ops.segment_sum(sent.reshape(PARTITIONS * TILES, BND, D), sources.reshape(-1), num_segments=PARTITIONS)
        local_sum = local_sum.at[part_index[:, None], boundary_rows].add(arrived)
        node_grad = self_part + local_sum.reshape(NODES, D)
    text_grad = node_grad[target]
    mean_grad = lax.optimization_barrier(jnp.mean(text_grad, axis=-1, keepdims=True))
    mean_cross = lax.optimization_barrier(jnp.mean(text_grad * normed, axis=-1, keepdims=True))
    dpooled = (inv_std * (text_grad - mean_grad - normed * mean_cross)).astype(jnp.bfloat16)
    down_grad = lead_contract(dpooled, text_hidden)
    return (node_out, text_grad, down_grad)
```

```python
import functools

import jax
import jax.numpy as jnp
import numpy as np
from jax import lax
from jax.experimental import pallas as pl
from jax.experimental.pallas import tpu as pltpu
from jax.sharding import PartitionSpec as P

SEQ = 8
TILES = 4
SPAN = 4
LAYERS = 2
LANES = 128
MESH = pl.DeviceIdType.MESH
BF16 = jnp.bfloat16
F32 = jnp.float32
INV_SQRT2 = float(np.sqrt(0.5))
INV_SQRT2PI = float(1.0 / np.sqrt(2.0 * np.pi))


def dot(left, right):
    return lax.dot_general(left, right, (((1,), (0,)), ((), ())), preferred_element_type=F32)


def dot_nt(left, right):
    return lax.dot_general(left, right, (((1,), (1,)), ((), ())), preferred_element_type=F32)


def gelu(x):
    return (0.5 * x) * (1.0 + lax.erf(x * INV_SQRT2))


def gelu_slope(x):
    return 0.5 * (1.0 + lax.erf(x * INV_SQRT2)) + x * (jnp.exp(-0.5 * x * x) * INV_SQRT2PI)


def rows_of(shape):
    return lax.broadcasted_iota(jnp.int32, shape, 0)


def cols_of(shape):
    return lax.broadcasted_iota(jnp.int32, shape, 1)


def one_hot(mask):
    return jnp.where(mask, 1.0, 0.0)


def eye(size):
    return one_hot(rows_of((size, size)) == cols_of((size, size))).astype(BF16)


def kernel(
    planes,
    texts,
    codes_ref,
    border_ref,
    peer_ref,
    tokens_hbm,
    up_hbm,
    down_hbm,
    feat_hbm,
    near_hbm,
    tile_hbm,
    self_hbm,
    neigh_hbm,
    cot_hbm,
    node_out,
    text_out,
    down_out,
    tokens,
    up,
    down,
    feat,
    near,
    tile,
    self_w,
    neigh_w,
    cot,
    self_x,
    neigh_x,
    pool_x,
    h_full,
    agg_full,
    gz_full,
    edge_out,
    edge_in,
    back_out,
    back_in,
    a1_out,
    a1_in,
    a2_out,
    a2_in,
    r1_out,
    r1_in,
    r2_out,
    r2_in,
    tg_full,
    dp_out,
    dp_in,
    th_all,
    rs_out,
    rs_in,
    pool_keep,
    normed_keep,
    pre_keep,
    tile_w,
    tile_t,
    near_t,
    border_t,
    border_m,
    inv_keep,
    place,
    place_t,
    swap_m,
    swap_t,
    send_m,
    send_t,
    load_sem,
    up_sem,
    wx_send,
    wx_recv,
    mp_send,
    mp_recv,
    edge_send,
    edge_recv,
    back_send,
    back_recv,
    all_send,
    all_recv,
    ring_send,
    ring_recv,
):
    dom = lax.axis_index("dom")
    core = lax.axis_index("mp")
    other = 1 - core
    domains = planes * a2_in.shape[0]
    spots = domains // planes
    z = dom // spots
    xy = lax.rem(dom, spots)
    half = feat.shape[1]
    nodes = feat.shape[0]
    bnd = edge_in.shape[2]
    pad = th_all.shape[1]
    sent_rows = -(-texts // 16) * 16

    loads = [
        pltpu.make_async_copy(src, dst, load_sem.at[i])
        for i, (src, dst) in enumerate(
            [
                (tokens_hbm, tokens),
                (down_hbm, down),
                (feat_hbm, feat),
                (near_hbm, near),
                (tile_hbm, tile),
                (self_hbm, self_w),
                (neigh_hbm, neigh_w),
                (cot_hbm, cot),
            ]
        )
    ]
    chunks, _, chunk = up.shape
    up_loads = [
        pltpu.make_async_copy(up_hbm.at[:, pl.ds(c * chunk, chunk)], up.at[c], up_sem.at[c])
        for c in range(chunks)
    ]
    loads[0].start()
    for load in up_loads:
        load.start()
    for load in loads[1:]:
        load.start()

    barrier = pltpu.get_barrier_semaphore()

    def greet(device, mp):
        pl.semaphore_signal(barrier, inc=1, device_id=(device, mp), device_id_type=MESH)

    greet(dom, other)
    for i in range(1, planes):
        greet(lax.rem(z + i, planes) * spots + xy, core)
    for i in range(1, spots):
        greet(z * spots + lax.rem(xy + i, spots), core)
    for o in range(1, SPAN + 1):
        greet(lax.rem(dom + o, domains), core)
        greet(lax.rem(dom + domains - o, domains), core)

    th_all[...] = jnp.zeros_like(th_all)
    rows = tokens.shape[0]
    mean_m = jnp.where(
        lax.shift_right_logical(cols_of((pad, rows)), 3) == rows_of((pad, rows)), 1.0 / SEQ, 0.0
    ).astype(BF16)
    loads[0].wait()
    for c in range(chunks):
        up_loads[c].wait()
        hidden = gelu(dot(tokens[...], up[c])).astype(BF16)
        mean_h = dot(mean_m, hidden).astype(BF16)
        th_all[z, :, pl.ds(c * chunk, chunk)] = mean_h
        if c == 0:
            loads[1].wait()
            pool_keep[...] = dot(mean_h, down[pl.ds(0, chunk), :])
        else:
            pool_keep[...] += dot(mean_h, down[pl.ds(c * chunk, chunk), :])

    pl.semaphore_wait(barrier, planes - 1 + spots - 1 + 2 * SPAN + 1)

    def to_core(src, dst, slot):
        copy = pltpu.make_async_remote_copy(
            src, dst, mp_send.at[slot], mp_recv.at[slot], device_id=(dom, other), device_id_type=MESH
        )
        copy.start()
        return copy

    pool_copy = to_core(pool_keep.at[pl.ds(0, texts)], pool_x.at[pl.ds(0, texts)], 0)
    swaps = []
    for kind, (src, dst) in enumerate([(self_hbm, self_x), (neigh_hbm, neigh_x)]):
        for layer in range(LAYERS):
            copy = pltpu.make_async_remote_copy(
                src.at[layer, pl.ds(pl.multiple_of(other * half, half), half)],
                dst.at[layer],
                wx_send.at[kind, layer],
                wx_recv.at[kind, layer],
                device_id=(dom, other),
                device_id_type=MESH,
            )
            copy.start()
            swaps.append(copy)

    upper = one_hot(rows_of((pad, pad)) < cols_of((pad, pad))).astype(BF16)
    mine = lax.shift_right_arithmetic(codes_ref[pl.ds(xy * planes + z, 1), :], 8)
    named = one_hot(rows_of((domains, pad)) == mine)
    earlier = dot(named.astype(BF16), upper)
    first = jnp.where(earlier < 0.5, named, 0.0).reshape(planes, spots, pad)
    second = jnp.where(earlier > 0.5, named, 0.0).reshape(planes, spots, pad)
    send_m[...] = jnp.concatenate([first, second], axis=1).reshape(2 * domains, pad).astype(BF16)
    token_mean = dot(mean_m, tokens[...])

    pool_copy.wait_recv()
    in_text = rows_of((pad, 1)) < texts
    pooled = token_mean + pool_keep[...] + jnp.where(in_text, pool_x[...], 0.0)
    centre = pooled - jnp.mean(pooled, axis=-1, keepdims=True)
    inv_std = lax.rsqrt(jnp.mean(centre * centre, axis=-1, keepdims=True) + 1e-05)
    normed = centre * inv_std
    normed_keep[...] = normed
    own = jnp.where(core == 0, normed[:, :half], normed[:, half:]).astype(BF16)
    a1_out[...] = dot(send_m[...], own).astype(BF16).reshape(a1_out.shape)

    def spread_z(src, dst, slot):
        for i in range(1, planes):
            to = lax.rem(z + i, planes)
            pltpu.make_async_remote_copy(
                src.at[to],
                dst.at[z],
                all_send.at[slot],
                all_recv.at[slot],
                device_id=(to * spots + xy, core),
                device_id_type=MESH,
            ).start()
        pltpu.make_async_copy(src.at[z], dst.at[z], all_recv.at[slot]).start()

    def spread_xy(src, dst, slot):
        for i in range(1, spots):
            to = lax.rem(xy + i, spots)
            pltpu.make_async_remote_copy(
                src.at[to],
                dst.at[xy],
                all_send.at[slot],
                all_recv.at[slot],
                device_id=(z * spots + to, core),
                device_id_type=MESH,
            ).start()
        pltpu.make_async_copy(src.at[xy], dst.at[xy], all_recv.at[slot]).start()

    def arrived(dst, slot):
        pltpu.make_async_copy(dst, dst, all_recv.at[slot]).wait()

    def left(src, slot):
        part = src.at[pl.ds(0, src.shape[0] - 1)]
        pltpu.make_async_copy(part, part, all_send.at[slot]).wait()

    spread_z(a1_out, a1_in, 0)

    codes = codes_ref[...]
    mask = lax.shift_right_arithmetic(codes, 8) == dom
    row = (codes & 255).astype(F32)
    before = dot(one_hot(mask).astype(BF16), upper)
    row0 = jnp.max(jnp.where(mask & (before < 0.5), row, -1.0), axis=1, keepdims=True)
    row1 = jnp.max(jnp.where(mask & (before > 0.5), row, -1.0), axis=1, keepdims=True)
    node = cols_of((domains, nodes)).astype(F32)
    at0 = one_hot(node == row0).reshape(spots, planes, nodes)
    at1 = one_hot(node == row1).reshape(spots, planes, nodes)
    place_t[...] = jnp.concatenate([at0, at1], axis=1).reshape(2 * domains, nodes).astype(BF16)
    place[...] = dot_nt(eye(nodes), place_t[...]).astype(BF16)
    square = (2 * domains, 2 * domains)

    def swapped(index, inner, outer):
        low = lax.rem(index, inner)
        slot = lax.rem(index // inner, 2)
        high = index // (2 * inner)
        return low * (2 * outer) + slot * outer + high

    swap_m[...] = one_hot(cols_of(square) == swapped(rows_of(square), planes, spots)).astype(BF16)
    swap_t[...] = one_hot(cols_of(square) == swapped(rows_of(square), spots, planes)).astype(BF16)
    send_t[...] = dot_nt(eye(pad), send_m[...]).astype(BF16)

    arrived(a1_in, 0)
    a2_out[...] = (
        dot(swap_m[...], a1_in[...].reshape(2 * domains, half)).astype(BF16).reshape(a2_out.shape)
    )
    spread_xy(a2_out, a2_in, 1)

    up_steps, down_steps = planes // 2, (planes - 1) // 2

    def ring(step, down_way):
        if down_way:
            block, to = lax.rem(z + step, planes), lax.rem(z + planes - 1, planes)
        else:
            block, to = lax.rem(z + planes - step, planes), lax.rem(z + 1, planes)
        view = th_all.at[block, pl.ds(0, sent_rows)]
        return pltpu.make_async_remote_copy(
            view,
            view,
            ring_send.at[int(down_way), step],
            ring_recv.at[int(down_way), step],
            device_id=(to * spots + xy, core),
            device_id_type=MESH,
        )

    def ring_arrive(step, down_way):
        if down_way:
            block = lax.rem(z + step + 1, planes)
        else:
            block = lax.rem(z + 2 * planes - step - 1, planes)
        view = th_all.at[block, pl.ds(0, sent_rows)]
        pltpu.make_async_copy(view, view, ring_recv.at[int(down_way), step]).wait()

    def ring_step(step):
        for down_way, steps in ((False, up_steps), (True, down_steps)):
            if 0 < step <= steps:
                ring_arrive(step - 1, down_way)
            if step < steps:
                ring(step, down_way).start()

    ring_step(0)

    for load in loads[2:]:
        load.wait()
    tall = tile.shape[0]
    for t in range(TILES):
        pick = one_hot(cols_of((nodes, tall)) == rows_of((nodes, tall)) * TILES + t).astype(BF16)
        tile_w[:, pl.ds(t * bnd, bnd)] = dot(pick, tile[...]).astype(BF16)
    for t in range(TILES):
        tile_t[pl.ds(t * bnd, bnd), :] = dot_nt(
            eye(bnd), tile_w[:, pl.ds(t * bnd, bnd)]
        ).astype(BF16)
    near_t[...] = dot_nt(eye(nodes), near[...]).astype(BF16)
    border = one_hot(rows_of((nodes, bnd)) == border_ref[...]).astype(BF16)
    for o in range(SPAN):
        border_m[:, pl.ds(o * bnd, bnd)] = border
    border_t[...] = dot_nt(eye(bnd), border).astype(BF16)
    degree = (
        1.0
        + dot(near[...], jnp.ones((nodes, half), BF16))
        + dot(tile_w[...], jnp.ones((TILES * bnd, half), BF16))
    )
    inv_keep[...] = 1.0 / degree

    arrived(a2_in, 1)
    state = (
        feat[...].astype(F32) + dot(place[...], a2_in[...].reshape(2 * domains, half))
    ).astype(BF16)

    own_k = pl.ds(pl.multiple_of(core * half, half), half)
    other_k = pl.ds(pl.multiple_of(other * half, half), half)
    h_copies, agg_copies, edge_copies = [], [], []
    for layer in range(LAYERS):
        h_full[layer, core] = state
        edge_out[layer] = dot(border_t[...], state).astype(BF16)
        sent = []
        for o in range(SPAN):
            copy = pltpu.make_async_remote_copy(
                edge_out.at[layer],
                edge_in.at[layer, o],
                edge_send.at[layer, o],
                edge_recv.at[layer, o],
                device_id=(lax.rem(dom + o + 1, domains), core),
                device_id_type=MESH,
            )
            copy.start()
            sent.append(copy)
        h_copy = to_core(h_full.at[layer, core], h_full.at[layer, core], 1 + layer)
        total = state.astype(F32) + dot(near[...], state)
        pre = dot(state, self_w[layer, own_k, :])
        pltpu.make_async_copy(
            h_full.at[layer, other], h_full.at[layer, other], mp_recv.at[1 + layer]
        ).wait()
        pre += dot(h_full[layer, other], self_w[layer, other_k, :])
        ring_step(layer + 1)
        for copy in sent:
            copy.wait_recv()
        for t in range(TILES):
            picked = edge_in[layer, 0]
            for o in range(1, SPAN):
                picked = jnp.where(peer_ref[0, t] == o, edge_in[layer, o], picked)
            total += dot(tile_w[:, pl.ds(t * bnd, bnd)], picked)
        agg = (total * inv_keep[...]).astype(BF16)
        agg_full[layer, core] = agg
        agg_copy = to_core(agg_full.at[layer, core], agg_full.at[layer, core], 3 + layer)
        pre += dot(agg, neigh_w[layer, own_k, :])
        pltpu.make_async_copy(
            agg_full.at[layer, other], agg_full.at[layer, other], mp_recv.at[3 + layer]
        ).wait()
        pre += dot(agg_full[layer, other], neigh_w[layer, other_k, :])
        pre_keep[layer] = pre
        state = gelu(pre).astype(BF16)
        h_copies.append(h_copy)
        agg_copies.append(agg_copy)
        edge_copies.extend(sent)
    node_out[...] = state

    for copy in swaps:
        copy.wait()
    grad = cot[...].astype(F32)
    gz_copies, back_copies = [], []
    for layer in reversed(range(LAYERS)):
        gz = (grad * gelu_slope(pre_keep[layer])).astype(BF16)
        gz_full[layer, core] = gz
        gz_copies.append(to_core(gz_full.at[layer, core], gz_full.at[layer, core], 5 + layer))
        self_part = dot_nt(gz, self_w[layer, own_k, :])
        mean_part = dot_nt(gz, neigh_w[layer, own_k, :])
        pltpu.make_async_copy(
            gz_full.at[layer, other], gz_full.at[layer, other], mp_recv.at[5 + layer]
        ).wait()
        gz_other = gz_full[layer, other]
        mean_part += dot_nt(gz_other, neigh_x[layer])
        scaled = (mean_part * inv_keep[...]).astype(BF16)
        pieces = [dot(tile_t[pl.ds(t * bnd, bnd), :], scaled) for t in range(TILES)]
        sent = []
        for o in range(SPAN):
            bundle = jnp.where(peer_ref[0, 0] == o, pieces[0], 0.0)
            for t in range(1, TILES):
                bundle += jnp.where(peer_ref[0, t] == o, pieces[t], 0.0)
            back_out[layer, o] = bundle.astype(BF16)
            copy = pltpu.make_async_remote_copy(
                back_out.at[layer, o],
                back_in.at[layer, o],
                back_send.at[layer, o],
                back_recv.at[layer, o],
                device_id=(lax.rem(dom + domains - o - 1, domains), core),
                device_id_type=MESH,
            )
            copy.start()
            sent.append(copy)
        self_part += dot_nt(gz_other, self_x[layer])
        grad = self_part + scaled.astype(F32) + dot(near_t[...], scaled)
        ring_step(LAYERS + LAYERS - layer)
        for copy in sent:
            copy.wait_recv()
        grad += dot(border_m[...], back_in[layer].reshape(SPAN * bnd, half))
        back_copies.extend(sent)

    r1_out[...] = dot(place_t[...], grad.astype(BF16)).astype(BF16).reshape(r1_out.shape)
    spread_xy(r1_out, r1_in, 2)
    arrived(r1_in, 2)
    r2_out[...] = (
        dot(swap_t[...], r1_in[...].reshape(2 * domains, half)).astype(BF16).reshape(r2_out.shape)
    )
    spread_z(r2_out, r2_in, 3)
    arrived(r2_in, 3)
    text_grad = dot(send_t[...], r2_in[...].reshape(2 * domains, half))
    tg_full[core] = text_grad.astype(BF16)
    tg_copy = to_core(tg_full.at[core], tg_full.at[core], 7)
    text_out[...] = text_grad[:texts]
    pltpu.make_async_copy(tg_full.at[other], tg_full.at[other], mp_recv.at[7]).wait()
    full = jnp.concatenate([tg_full[0], tg_full[1]], axis=1).astype(F32)
    normed = normed_keep[...]
    mean_grad = jnp.mean(full, axis=-1, keepdims=True)
    mean_cross = jnp.mean(full * normed, axis=-1, keepdims=True)
    dpooled = inv_std * (full - mean_grad - normed * mean_cross)
    dp_out[...] = dpooled.T.astype(BF16).reshape(dp_out.shape)
    spread_z(dp_out, dp_in, 4)

    slab = dp_in.shape[1]
    share = slab // spots
    room = rs_in.shape[1] // 2
    spread = (spots * room, slab)
    row_at = lax.rem(rows_of(spread), room)
    pick = one_hot(
        (row_at < share) & (cols_of(spread) == rows_of(spread) // room * share + row_at)
    ).astype(BF16)
    arrived(dp_in, 4)
    joined = jnp.concatenate([dp_in[i] for i in range(planes)], axis=1)
    joined = dot(pick, joined).astype(BF16)
    means = th_all[...].reshape(planes * pad, th_all.shape[2])
    part = dot(joined, means)
    cut = part.shape[1] // 2
    rs_out[...] = jnp.concatenate(
        [part[:, :cut].reshape(spots, room, cut), part[:, cut:].reshape(spots, room, cut)], axis=1
    ).astype(BF16)
    spread_xy(rs_out, rs_in, 5)
    arrived(rs_in, 5)
    total = jnp.sum(rs_in[...].astype(F32), axis=0)
    down_out[:, pl.ds(0, cut)] = total[:share]
    down_out[:, pl.ds(cut, cut)] = total[room : room + share]

    pool_copy.wait_send()
    for copy in h_copies + agg_copies + edge_copies + gz_copies + back_copies + [tg_copy]:
        copy.wait_send()
    for slot, src in enumerate((a1_out, a2_out, r1_out, r2_out, dp_out, rs_out)):
        left(src, slot)
    for down_way, steps in ((False, up_steps), (True, down_steps)):
        for step in range(steps):
            ring(step, down_way).wait_send()


def local(
    tokens,
    up_weight,
    down_weight,
    text_owner,
    text_row,
    node_feat,
    local_weight,
    tile_weight,
    tile_peer,
    boundary_rows,
    self_weight,
    neigh_weight,
    node_cot,
    planes,
):
    domains = lax.axis_size("dom")
    spots = domains // planes
    rows, width = tokens.shape
    texts = rows // SEQ
    pad = -(-texts // LANES) * LANES
    nodes, half = node_feat.shape
    bnd = boundary_rows.shape[1]
    hidden = up_weight.shape[1]
    chunk = min(256, hidden)
    chunks = hidden // chunk
    share = width // domains
    room = -(-share // 8) * 8
    slab = width // planes

    codes = (text_owner.reshape(-1) * 256 + text_row).reshape(planes, spots, texts)
    codes = jnp.pad(
        codes.transpose(1, 0, 2).reshape(domains, texts),
        ((0, 0), (0, pad - texts)),
        constant_values=-1,
    )
    tile = tile_weight.reshape(nodes * TILES, bnd)

    def vm(*shape, dtype=BF16):
        return pltpu.VMEM(shape, dtype)

    dma = pltpu.SemaphoreType.DMA
    scratch = [
        vm(rows, width),
        vm(chunks, width, chunk),
        vm(hidden, width),
        vm(nodes, half),
        vm(nodes, nodes),
        vm(nodes * TILES, bnd),
        vm(LAYERS, width, half),
        vm(LAYERS, width, half),
        vm(nodes, half),
        vm(LAYERS, half, half),
        vm(LAYERS, half, half),
        vm(pad, width, dtype=F32),
        vm(LAYERS, 2, nodes, half),
        vm(LAYERS, 2, nodes, half),
        vm(LAYERS, 2, nodes, half),
        vm(LAYERS, bnd, half),
        vm(LAYERS, SPAN, bnd, half),
        vm(LAYERS, SPAN, bnd, half),
        vm(LAYERS, SPAN, bnd, half),
        vm(planes, 2 * spots, half),
        vm(planes, 2 * spots, half),
        vm(spots, 2 * planes, half),
        vm(spots, 2 * planes, half),
        vm(spots, 2 * planes, half),
        vm(spots, 2 * planes, half),
        vm(planes, 2 * spots, half),
        vm(planes, 2 * spots, half),
        vm(2, pad, half),
        vm(planes, slab, pad),
        vm(planes, slab, pad),
        vm(planes, pad, hidden),
        vm(spots, 2 * room, hidden // 2),
        vm(spots, 2 * room, hidden // 2),
        vm(pad, width, dtype=F32),
        vm(pad, width, dtype=F32),
        vm(LAYERS, nodes, half, dtype=F32),
        vm(nodes, TILES * bnd),
        vm(TILES * bnd, nodes),
        vm(nodes, nodes),
        vm(bnd, nodes),
        vm(nodes, SPAN * bnd),
        vm(nodes, half, dtype=F32),
        vm(nodes, 2 * domains),
        vm(2 * domains, nodes),
        vm(2 * domains, 2 * domains),
        vm(2 * domains, 2 * domains),
        vm(2 * domains, pad),
        vm(pad, 2 * domains),
        dma((8,)),
        dma((chunks,)),
        dma((2, LAYERS)),
        dma((2, LAYERS)),
        dma((8,)),
        dma((8,)),
        dma((LAYERS, SPAN)),
        dma((LAYERS, SPAN)),
        dma((LAYERS, SPAN)),
        dma((LAYERS, SPAN)),
        dma((6,)),
        dma((6,)),
        dma((2, max(1, planes // 2))),
        dma((2, max(1, planes // 2))),
    ]
    vmem = pl.BlockSpec(memory_space=pltpu.VMEM)
    smem = pl.BlockSpec(memory_space=pltpu.SMEM)
    hbm = pl.BlockSpec(memory_space=pl.ANY)
    return pl.pallas_call(
        functools.partial(kernel, planes, texts),
        out_shape=(
            jax.ShapeDtypeStruct((nodes, half), BF16),
            jax.ShapeDtypeStruct((texts, half), F32),
            jax.ShapeDtypeStruct((share, hidden), F32),
        ),
        in_specs=[vmem, vmem, smem] + [hbm] * 9,
        out_specs=(vmem, vmem, vmem),
        scratch_shapes=scratch,
        compiler_params=pltpu.CompilerParams(
            collective_id=0, has_side_effects=True, vmem_limit_bytes=58 * 2**20
        ),
    )(
        codes,
        boundary_rows,
        tile_peer,
        tokens,
        up_weight,
        down_weight,
        node_feat,
        local_weight,
        tile,
        self_weight,
        neigh_weight,
        node_cot,
    )


def solution(mesh):
    in_specs = (
        P("dom", None),
        P(None, "mp"),
        P("mp", None),
        P(),
        P(),
        P("dom", "mp"),
        P("dom", None),
        P("dom", None, None),
        P("dom", None),
        P("dom", None),
        P(None, None, "mp"),
        P(None, None, "mp"),
        P("dom", "mp"),
    )
    out_specs = (P("dom", "mp"), P("dom", "mp"), P("dom", "mp"))
    domains = mesh.shape["dom"]
    planes = 8 if domains >= 128 else 2
    return jax.shard_map(
        functools.partial(local, planes=planes),
        mesh=mesh,
        in_specs=in_specs,
        out_specs=out_specs,
        check_vma=False,
    )
```

```python
import functools

import jax
import jax.numpy as jnp
import numpy as np
from jax import lax
from jax.experimental import pallas as pl
from jax.experimental.pallas import tpu as pltpu
from jax.sharding import PartitionSpec as P

SEQ = 8
TILES = 4
SPAN = 4
LAYERS = 2
LANES = 128
MESH = pl.DeviceIdType.MESH
BF16 = jnp.bfloat16
F32 = jnp.float32
INV_SQRT2 = float(np.sqrt(0.5))
INV_SQRT2PI = float(1.0 / np.sqrt(2.0 * np.pi))


def dot(left, right):
    return lax.dot_general(left, right, (((1,), (0,)), ((), ())), preferred_element_type=F32)


def dot_nt(left, right):
    return lax.dot_general(left, right, (((1,), (1,)), ((), ())), preferred_element_type=F32)


def gelu(x):
    return (0.5 * x) * (1.0 + lax.erf(x * INV_SQRT2))


def gelu_slope(x):
    return 0.5 * (1.0 + lax.erf(x * INV_SQRT2)) + x * (jnp.exp(-0.5 * x * x) * INV_SQRT2PI)


def rows_of(shape):
    return lax.broadcasted_iota(jnp.int32, shape, 0)


def cols_of(shape):
    return lax.broadcasted_iota(jnp.int32, shape, 1)


def one_hot(mask):
    return jnp.where(mask, 1.0, 0.0)


def eye(size):
    return one_hot(rows_of((size, size)) == cols_of((size, size))).astype(BF16)


def kernel(
    planes,
    texts,
    owner_ref,
    row_ref,
    border_ref,
    peer_ref,
    tokens_hbm,
    up_hbm,
    down_hbm,
    feat_hbm,
    near_hbm,
    tile_hbm,
    self_hbm,
    neigh_hbm,
    cot_hbm,
    node_out,
    text_out,
    down_out,
    tokens,
    up,
    down,
    feat,
    near,
    tile,
    self_w,
    neigh_w,
    cot,
    self_x,
    neigh_x,
    pool_x,
    h_full,
    agg_full,
    gz_full,
    edge_out,
    edge_in,
    back_out,
    back_in,
    a1_out,
    a1_in,
    a2_out,
    a2_in,
    r1_out,
    r1_in,
    r2_out,
    r2_in,
    tg_full,
    dp_out,
    dp_in,
    th_all,
    rs_out,
    rs_in,
    owner_keep,
    pool_keep,
    normed_keep,
    pre_keep,
    tile_w,
    tile_t,
    near_t,
    border_t,
    border_m,
    inv_keep,
    place,
    place_t,
    swap_m,
    swap_t,
    send_m,
    send_t,
    load_sem,
    up_sem,
    down_sem,
    wx_send,
    wx_recv,
    mp_send,
    mp_recv,
    edge_send,
    edge_recv,
    back_send,
    back_recv,
    all_send,
    all_recv,
    ring_send,
    ring_recv,
):
    dom = lax.axis_index("dom")
    core = lax.axis_index("mp")
    other = 1 - core
    domains = planes * a2_in.shape[0]
    spots = domains // planes
    z = dom // spots
    xy = lax.rem(dom, spots)
    half = feat.shape[1]
    nodes = feat.shape[0]
    bnd = edge_in.shape[2]
    pad = th_all.shape[1]
    sent_rows = -(-texts // 16) * 16

    loads = [
        pltpu.make_async_copy(src, dst, load_sem.at[i])
        for i, (src, dst) in enumerate(
            [
                (tokens_hbm, tokens),
                (feat_hbm, feat),
                (near_hbm, near),
                (tile_hbm, tile),
                (self_hbm, self_w),
                (neigh_hbm, neigh_w),
                (cot_hbm, cot),
            ]
        )
    ]
    chunks, _, chunk = up.shape
    up_loads = [
        pltpu.make_async_copy(up_hbm.at[:, pl.ds(c * chunk, chunk)], up.at[c], up_sem.at[c])
        for c in range(chunks)
    ]
    down_loads = [
        pltpu.make_async_copy(
            down_hbm.at[pl.ds(c * chunk, chunk), :],
            down.at[pl.ds(c * chunk, chunk), :],
            down_sem.at[c],
        )
        for c in range(chunks)
    ]
    loads[0].start()
    for c in range(chunks):
        up_loads[c].start()
        down_loads[c].start()
    for load in loads[1:]:
        load.start()

    barrier = pltpu.get_barrier_semaphore()

    def greet(device, mp):
        pl.semaphore_signal(barrier, inc=1, device_id=(device, mp), device_id_type=MESH)

    greet(dom, other)
    for i in range(1, planes):
        greet(lax.rem(z + i, planes) * spots + xy, core)
    for i in range(1, spots):
        greet(z * spots + lax.rem(xy + i, spots), core)
    for o in range(1, SPAN + 1):
        greet(lax.rem(dom + o, domains), core)
        greet(lax.rem(dom + domains - o, domains), core)

    up_steps, down_steps = planes // 2, (planes - 1) // 2
    ring_plan = [
        [(step, c) for step in range(steps) for c in range(chunks)] for steps in (up_steps, down_steps)
    ]
    ring_done = [0, 0]

    def ring(way, step, c):
        if way:
            block, to = lax.rem(z + step, planes), lax.rem(z + planes - 1, planes)
        else:
            block, to = lax.rem(z + planes - step, planes), lax.rem(z + 1, planes)
        view = th_all.at[block, pl.ds(0, sent_rows), pl.ds(c * chunk, chunk)]
        return pltpu.make_async_remote_copy(
            view,
            view,
            ring_send.at[way, step, c],
            ring_recv.at[way, step, c],
            device_id=(to * spots + xy, core),
            device_id_type=MESH,
        )

    def ring_arrive(way, step, c):
        if way:
            block = lax.rem(z + step + 1, planes)
        else:
            block = lax.rem(z + 2 * planes - step - 1, planes)
        view = th_all.at[block, pl.ds(0, sent_rows), pl.ds(c * chunk, chunk)]
        pltpu.make_async_copy(view, view, ring_recv.at[way, step, c]).wait()

    def ring_advance(way, count):
        for step, c in ring_plan[way][ring_done[way] : ring_done[way] + count]:
            if step > 0:
                ring_arrive(way, step - 1, c)
            ring(way, step, c).start()
            ring_done[way] += 1

    th_all[:, pl.ds(sent_rows, pad - sent_rows), :] = jnp.zeros(
        (planes, pad - sent_rows, th_all.shape[2]), BF16
    )
    rows = tokens.shape[0]
    mean_m = jnp.where(
        lax.shift_right_logical(cols_of((pad, rows)), 3) == rows_of((pad, rows)), 1.0 / SEQ, 0.0
    ).astype(BF16)
    loads[0].wait()
    for c in range(chunks):
        up_loads[c].wait()
        hidden = gelu(dot(tokens[...], up[c])).astype(BF16)
        mean_h = dot(mean_m, hidden).astype(BF16)
        th_all[z, :, pl.ds(c * chunk, chunk)] = mean_h
        down_loads[c].wait()
        partial = dot(mean_h, down[pl.ds(c * chunk, chunk), :])
        if c == 0:
            pool_keep[...] = partial
            pl.semaphore_wait(barrier, planes - 1 + spots - 1 + 2 * SPAN + 1)
        else:
            pool_keep[...] += partial
        ring_advance(0, 1)
        ring_advance(1, 1)

    def to_core(src, dst, slot):
        copy = pltpu.make_async_remote_copy(
            src, dst, mp_send.at[slot], mp_recv.at[slot], device_id=(dom, other), device_id_type=MESH
        )
        copy.start()
        return copy

    pool_copy = to_core(pool_keep.at[pl.ds(0, texts)], pool_x.at[pl.ds(0, texts)], 0)
    swaps = []
    for kind, (src, dst) in enumerate([(self_hbm, self_x), (neigh_hbm, neigh_x)]):
        for layer in range(LAYERS):
            copy = pltpu.make_async_remote_copy(
                src.at[layer, pl.ds(pl.multiple_of(other * half, half), half)],
                dst.at[layer],
                wx_send.at[kind, layer],
                wx_recv.at[kind, layer],
                device_id=(dom, other),
                device_id_type=MESH,
            )
            copy.start()
            swaps.append(copy)

    ring_advance(0, 1)
    ring_advance(1, 1)
    lines, lanes = owner_ref.shape
    line_of = rows_of((domains, lines)) * texts // lanes
    low = one_hot(cols_of((domains, lines)) == line_of).astype(BF16)
    high = one_hot(cols_of((domains, lines)) == line_of + 1).astype(BF16)
    shard = (domains, lanes)
    inside = cols_of(shard) + lax.rem(rows_of(shard) * texts, lanes) < lanes

    def by_shard(ref):
        flat = ref[...].astype(F32).astype(BF16)
        turned = [dot(m, flat) for m in (low, high)]
        for bit in range(lanes.bit_length() - 1):
            shift = (lanes - texts) * 2**bit % lanes
            if shift:
                moved = lax.rem(rows_of(shard) // 2**bit, 2) == 1
                turned = [jnp.where(moved, pltpu.roll(m, shift, 1), m) for m in turned]
        return jnp.where(cols_of(shard) < texts, jnp.where(inside, *turned), -1.0)

    owner_of = by_shard(owner_ref)
    row_of = by_shard(row_ref)
    owner_keep[...] = owner_of

    upper = one_hot(rows_of((pad, pad)) < cols_of((pad, pad))).astype(BF16)
    mine = owner_keep[pl.ds(dom, 1), :]
    named = one_hot(rows_of((domains, pad)).astype(F32) == mine)
    earlier = dot(named.astype(BF16), upper)
    first = jnp.where(earlier < 0.5, named, 0.0).reshape(planes, spots, pad)
    second = jnp.where(earlier > 0.5, named, 0.0).reshape(planes, spots, pad)
    send_m[...] = jnp.concatenate([first, second], axis=1).reshape(2 * domains, pad).astype(BF16)
    token_mean = dot(mean_m, tokens[...])

    pool_copy.wait_recv()
    in_text = rows_of((pad, 1)) < texts
    pooled = token_mean + pool_keep[...] + jnp.where(in_text, pool_x[...], 0.0)
    centre = pooled - jnp.mean(pooled, axis=-1, keepdims=True)
    inv_std = lax.rsqrt(jnp.mean(centre * centre, axis=-1, keepdims=True) + 1e-05)
    normed = centre * inv_std
    normed_keep[...] = normed
    own = jnp.where(core == 0, normed[:, :half], normed[:, half:]).astype(BF16)
    a1_out[...] = dot(send_m[...], own).astype(BF16).reshape(a1_out.shape)

    def spread_z(src, dst, slot):
        for i in range(1, planes):
            to = lax.rem(z + i, planes)
            pltpu.make_async_remote_copy(
                src.at[to],
                dst.at[z],
                all_send.at[slot],
                all_recv.at[slot],
                device_id=(to * spots + xy, core),
                device_id_type=MESH,
            ).start()
        pltpu.make_async_copy(src.at[z], dst.at[z], all_recv.at[slot]).start()

    def spread_xy(src, dst, slot):
        for i in range(1, spots):
            to = lax.rem(xy + i, spots)
            pltpu.make_async_remote_copy(
                src.at[to],
                dst.at[xy],
                all_send.at[slot],
                all_recv.at[slot],
                device_id=(z * spots + to, core),
                device_id_type=MESH,
            ).start()
        pltpu.make_async_copy(src.at[xy], dst.at[xy], all_recv.at[slot]).start()

    def arrived(dst, slot):
        pltpu.make_async_copy(dst, dst, all_recv.at[slot]).wait()

    def left(src, slot):
        part = src.at[pl.ds(0, src.shape[0] - 1)]
        pltpu.make_async_copy(part, part, all_send.at[slot]).wait()

    spread_z(a1_out, a1_in, 0)

    mask = owner_of == dom.astype(F32)
    before = dot(one_hot(mask).astype(BF16), upper)
    row0 = jnp.max(jnp.where(mask & (before < 0.5), row_of, -1.0), axis=1, keepdims=True)
    row1 = jnp.max(jnp.where(mask & (before > 0.5), row_of, -1.0), axis=1, keepdims=True)
    node = cols_of((domains, nodes)).astype(F32)
    at0 = one_hot(node == row0).reshape(planes, spots, nodes)
    at1 = one_hot(node == row1).reshape(planes, spots, nodes)
    square = (2 * domains, 2 * domains)

    def swapped(index, inner, outer):
        low = lax.rem(index, inner)
        slot = lax.rem(index // inner, 2)
        high = index // (2 * inner)
        return low * (2 * outer) + slot * outer + high

    swap_m[...] = one_hot(cols_of(square) == swapped(rows_of(square), planes, spots)).astype(BF16)
    swap_t[...] = one_hot(cols_of(square) == swapped(rows_of(square), spots, planes)).astype(BF16)
    at = jnp.concatenate([at0, at1], axis=1).reshape(2 * domains, nodes).astype(BF16)
    place_t[...] = dot(swap_m[...], at).astype(BF16)
    place[...] = dot_nt(eye(nodes), place_t[...]).astype(BF16)
    send_t[...] = dot_nt(eye(pad), send_m[...]).astype(BF16)

    arrived(a1_in, 0)
    a2_out[...] = (
        dot(swap_m[...], a1_in[...].reshape(2 * domains, half)).astype(BF16).reshape(a2_out.shape)
    )
    spread_xy(a2_out, a2_in, 1)

    ring_advance(0, 2)
    ring_advance(1, 2)

    for load in loads[1:]:
        load.wait()
    tall = tile.shape[0]
    for t in range(TILES):
        pick = one_hot(cols_of((nodes, tall)) == rows_of((nodes, tall)) * TILES + t).astype(BF16)
        tile_w[:, pl.ds(t * bnd, bnd)] = dot(pick, tile[...]).astype(BF16)
    for t in range(TILES):
        tile_t[pl.ds(t * bnd, bnd), :] = dot_nt(
            eye(bnd), tile_w[:, pl.ds(t * bnd, bnd)]
        ).astype(BF16)
    near_t[...] = dot_nt(eye(nodes), near[...]).astype(BF16)
    border = one_hot(rows_of((nodes, bnd)) == border_ref[...]).astype(BF16)
    for o in range(SPAN):
        border_m[:, pl.ds(o * bnd, bnd)] = border
    border_t[...] = dot_nt(eye(bnd), border).astype(BF16)
    degree = (
        1.0
        + dot(near[...], jnp.ones((nodes, half), BF16))
        + dot(tile_w[...], jnp.ones((TILES * bnd, half), BF16))
    )
    inv_keep[...] = 1.0 / degree

    arrived(a2_in, 1)
    state = (
        feat[...].astype(F32) + dot(place[...], a2_in[...].reshape(2 * domains, half))
    ).astype(BF16)

    own_k = pl.ds(pl.multiple_of(core * half, half), half)
    other_k = pl.ds(pl.multiple_of(other * half, half), half)
    h_copies, agg_copies, edge_copies = [], [], []
    for layer in range(LAYERS):
        h_full[layer, core] = state
        edge_out[layer] = dot(border_t[...], state).astype(BF16)
        sent = []
        for o in range(SPAN):
            copy = pltpu.make_async_remote_copy(
                edge_out.at[layer],
                edge_in.at[layer, o],
                edge_send.at[layer, o],
                edge_recv.at[layer, o],
                device_id=(lax.rem(dom + o + 1, domains), core),
                device_id_type=MESH,
            )
            copy.start()
            sent.append(copy)
        h_copy = to_core(h_full.at[layer, core], h_full.at[layer, core], 1 + layer)
        total = state.astype(F32) + dot(near[...], state)
        pre = dot(state, self_w[layer, own_k, :])
        pltpu.make_async_copy(
            h_full.at[layer, other], h_full.at[layer, other], mp_recv.at[1 + layer]
        ).wait()
        pre += dot(h_full[layer, other], self_w[layer, other_k, :])
        ring_advance(0, 1)
        ring_advance(1, 2)
        for copy in sent:
            copy.wait_recv()
        for t in range(TILES):
            picked = edge_in[layer, 0]
            for o in range(1, SPAN):
                picked = jnp.where(peer_ref[0, t] == o, edge_in[layer, o], picked)
            total += dot(tile_w[:, pl.ds(t * bnd, bnd)], picked)
        agg = (total * inv_keep[...]).astype(BF16)
        agg_full[layer, core] = agg
        agg_copy = to_core(agg_full.at[layer, core], agg_full.at[layer, core], 3 + layer)
        pre += dot(agg, neigh_w[layer, own_k, :])
        pltpu.make_async_copy(
            agg_full.at[layer, other], agg_full.at[layer, other], mp_recv.at[3 + layer]
        ).wait()
        pre += dot(agg_full[layer, other], neigh_w[layer, other_k, :])
        pre_keep[layer] = pre
        state = gelu(pre).astype(BF16)
        h_copies.append(h_copy)
        agg_copies.append(agg_copy)
        edge_copies.extend(sent)
    node_out[...] = state

    for copy in swaps:
        copy.wait()
    grad = cot[...].astype(F32)
    gz_copies, back_copies = [], []
    for layer in reversed(range(LAYERS)):
        gz = (grad * gelu_slope(pre_keep[layer])).astype(BF16)
        gz_full[layer, core] = gz
        gz_copies.append(to_core(gz_full.at[layer, core], gz_full.at[layer, core], 5 + layer))
        self_part = dot_nt(gz, self_w[layer, own_k, :])
        mean_part = dot_nt(gz, neigh_w[layer, own_k, :])
        pltpu.make_async_copy(
            gz_full.at[layer, other], gz_full.at[layer, other], mp_recv.at[5 + layer]
        ).wait()
        gz_other = gz_full[layer, other]
        mean_part += dot_nt(gz_other, neigh_x[layer])
        scaled = (mean_part * inv_keep[...]).astype(BF16)
        pieces = [dot(tile_t[pl.ds(t * bnd, bnd), :], scaled) for t in range(TILES)]
        sent = []
        for o in range(SPAN):
            bundle = jnp.where(peer_ref[0, 0] == o, pieces[0], 0.0)
            for t in range(1, TILES):
                bundle += jnp.where(peer_ref[0, t] == o, pieces[t], 0.0)
            back_out[layer, o] = bundle.astype(BF16)
            copy = pltpu.make_async_remote_copy(
                back_out.at[layer, o],
                back_in.at[layer, o],
                back_send.at[layer, o],
                back_recv.at[layer, o],
                device_id=(lax.rem(dom + domains - o - 1, domains), core),
                device_id_type=MESH,
            )
            copy.start()
            sent.append(copy)
        self_part += dot_nt(gz_other, self_x[layer])
        grad = self_part + scaled.astype(F32) + dot(near_t[...], scaled)
        ring_advance(0, 2)
        for copy in sent:
            copy.wait_recv()
        grad += dot(border_m[...], back_in[layer].reshape(SPAN * bnd, half))
        back_copies.extend(sent)

    r1_out[...] = dot(place_t[...], grad.astype(BF16)).astype(BF16).reshape(r1_out.shape)
    spread_xy(r1_out, r1_in, 2)
    ring_advance(0, len(ring_plan[0]))
    ring_advance(1, len(ring_plan[1]))
    arrived(r1_in, 2)
    r2_out[...] = (
        dot(swap_t[...], r1_in[...].reshape(2 * domains, half)).astype(BF16).reshape(r2_out.shape)
    )
    spread_z(r2_out, r2_in, 3)
    arrived(r2_in, 3)
    text_grad = dot(send_t[...], r2_in[...].reshape(2 * domains, half))
    tg_full[core] = text_grad.astype(BF16)
    tg_copy = to_core(tg_full.at[core], tg_full.at[core], 7)
    text_out[...] = text_grad[:texts]
    pltpu.make_async_copy(tg_full.at[other], tg_full.at[other], mp_recv.at[7]).wait()
    full = jnp.concatenate([tg_full[0], tg_full[1]], axis=1).astype(F32)
    normed = normed_keep[...]
    mean_grad = jnp.mean(full, axis=-1, keepdims=True)
    mean_cross = jnp.mean(full * normed, axis=-1, keepdims=True)
    dpooled = inv_std * (full - mean_grad - normed * mean_cross)
    dp_out[...] = dpooled.T.astype(BF16).reshape(dp_out.shape)
    spread_z(dp_out, dp_in, 4)

    slab = dp_in.shape[1]
    share = slab // spots
    room = rs_in.shape[1] // 2
    spread = (spots * room, slab)
    row_at = lax.rem(rows_of(spread), room)
    pick = one_hot(
        (row_at < share) & (cols_of(spread) == rows_of(spread) // room * share + row_at)
    ).astype(BF16)
    arrived(dp_in, 4)
    for way, steps in ((0, up_steps), (1, down_steps)):
        for c in range(chunks if steps else 0):
            ring_arrive(way, steps - 1, c)
    joined = jnp.concatenate([dp_in[i] for i in range(planes)], axis=1)
    joined = dot(pick, joined).astype(BF16)
    means = th_all[...].reshape(planes * pad, th_all.shape[2])
    part = dot(joined, means)
    cut = part.shape[1] // 2
    rs_out[...] = jnp.concatenate(
        [part[:, :cut].reshape(spots, room, cut), part[:, cut:].reshape(spots, room, cut)], axis=1
    ).astype(BF16)
    spread_xy(rs_out, rs_in, 5)
    arrived(rs_in, 5)
    total = jnp.sum(rs_in[...].astype(F32), axis=0)
    down_out[:, pl.ds(0, cut)] = total[:share]
    down_out[:, pl.ds(cut, cut)] = total[room : room + share]

    pool_copy.wait_send()
    for copy in h_copies + agg_copies + edge_copies + gz_copies + back_copies + [tg_copy]:
        copy.wait_send()
    for slot, src in enumerate((a1_out, a2_out, r1_out, r2_out, dp_out, rs_out)):
        left(src, slot)
    for way in (0, 1):
        for step, c in ring_plan[way]:
            ring(way, step, c).wait_send()


def finish(node_ref, text_ref, down_ref, node_out, text_out, down_out):
    node_out[...] = node_ref[...]
    text_out[...] = text_ref[...]
    down_out[...] = down_ref[...]


def local(
    tokens,
    up_weight,
    down_weight,
    text_owner,
    text_row,
    node_feat,
    local_weight,
    tile_weight,
    tile_peer,
    boundary_rows,
    self_weight,
    neigh_weight,
    node_cot,
    planes,
):
    domains = lax.axis_size("dom")
    spots = domains // planes
    rows, width = tokens.shape
    texts = rows // SEQ
    pad = -(-texts // LANES) * LANES
    nodes, half = node_feat.shape
    bnd = boundary_rows.shape[1]
    hidden = up_weight.shape[1]
    chunk = min(512, hidden)
    chunks = hidden // chunk
    share = width // domains
    room = -(-share // 8) * 8
    slab = width // planes

    owners = text_owner.reshape(-1, LANES)
    text_rows = text_row.reshape(-1, LANES)
    tile = tile_weight.reshape(nodes * TILES, bnd)

    def vm(*shape, dtype=BF16):
        return pltpu.VMEM(shape, dtype)

    dma = pltpu.SemaphoreType.DMA
    scratch = [
        vm(rows, width),
        vm(chunks, width, chunk),
        vm(hidden, width),
        vm(nodes, half),
        vm(nodes, nodes),
        vm(nodes * TILES, bnd),
        vm(LAYERS, width, half),
        vm(LAYERS, width, half),
        vm(nodes, half),
        vm(LAYERS, half, half),
        vm(LAYERS, half, half),
        vm(pad, width, dtype=F32),
        vm(LAYERS, 2, nodes, half),
        vm(LAYERS, 2, nodes, half),
        vm(LAYERS, 2, nodes, half),
        vm(LAYERS, bnd, half),
        vm(LAYERS, SPAN, bnd, half),
        vm(LAYERS, SPAN, bnd, half),
        vm(LAYERS, SPAN, bnd, half),
        vm(planes, 2 * spots, half),
        vm(planes, 2 * spots, half),
        vm(spots, 2 * planes, half),
        vm(spots, 2 * planes, half),
        vm(spots, 2 * planes, half),
        vm(spots, 2 * planes, half),
        vm(planes, 2 * spots, half),
        vm(planes, 2 * spots, half),
        vm(2, pad, half),
        vm(planes, slab, pad),
        vm(planes, slab, pad),
        vm(planes, pad, hidden),
        vm(spots, 2 * room, hidden // 2),
        vm(spots, 2 * room, hidden // 2),
        vm(domains, LANES, dtype=F32),
        vm(pad, width, dtype=F32),
        vm(pad, width, dtype=F32),
        vm(LAYERS, nodes, half, dtype=F32),
        vm(nodes, TILES * bnd),
        vm(TILES * bnd, nodes),
        vm(nodes, nodes),
        vm(bnd, nodes),
        vm(nodes, SPAN * bnd),
        vm(nodes, half, dtype=F32),
        vm(nodes, 2 * domains),
        vm(2 * domains, nodes),
        vm(2 * domains, 2 * domains),
        vm(2 * domains, 2 * domains),
        vm(2 * domains, pad),
        vm(pad, 2 * domains),
        dma((7,)),
        dma((chunks,)),
        dma((chunks,)),
        dma((2, LAYERS)),
        dma((2, LAYERS)),
        dma((8,)),
        dma((8,)),
        dma((LAYERS, SPAN)),
        dma((LAYERS, SPAN)),
        dma((LAYERS, SPAN)),
        dma((LAYERS, SPAN)),
        dma((6,)),
        dma((6,)),
        dma((2, max(1, planes // 2), chunks)),
        dma((2, max(1, planes // 2), chunks)),
    ]
    vmem = pl.BlockSpec(memory_space=pltpu.VMEM)
    smem = pl.BlockSpec(memory_space=pltpu.SMEM)
    hbm = pl.BlockSpec(memory_space=pl.ANY)
    out_shape = (
        jax.ShapeDtypeStruct((nodes, half), BF16),
        jax.ShapeDtypeStruct((texts, half), F32),
        jax.ShapeDtypeStruct((share, hidden), F32),
    )
    results = pl.pallas_call(
        functools.partial(kernel, planes, texts),
        out_shape=out_shape,
        in_specs=[vmem, vmem, vmem, smem] + [hbm] * 9,
        out_specs=(vmem, vmem, vmem),
        scratch_shapes=scratch,
        compiler_params=pltpu.CompilerParams(
            collective_id=0, has_side_effects=True, vmem_limit_bytes=58 * 2**20
        ),
    )(
        owners,
        text_rows,
        boundary_rows,
        tile_peer,
        tokens,
        up_weight,
        down_weight,
        node_feat,
        local_weight,
        tile,
        self_weight,
        neigh_weight,
        node_cot,
    )
    return pl.pallas_call(
        finish,
        out_shape=out_shape,
        in_specs=[vmem] * 3,
        out_specs=(vmem,) * 3,
    )(*results)


def solution(mesh):
    in_specs = (
        P("dom", None),
        P(None, "mp"),
        P("mp", None),
        P(),
        P(),
        P("dom", "mp"),
        P("dom", None),
        P("dom", None, None),
        P("dom", None),
        P("dom", None),
        P(None, None, "mp"),
        P(None, None, "mp"),
        P("dom", "mp"),
    )
    out_specs = (P("dom", "mp"), P("dom", "mp"), P("dom", "mp"))
    domains = mesh.shape["dom"]
    planes = 8 if domains >= 128 else 2
    return jax.shard_map(
        functools.partial(local, planes=planes),
        mesh=mesh,
        in_specs=in_specs,
        out_specs=out_specs,
        check_vma=False,
    )
```

```python
import functools
import math

import jax
import jax.numpy as jnp
import numpy as np
from jax import lax
from jax.experimental import pallas as pl
from jax.experimental.pallas import tpu as pltpu
from jax.sharding import PartitionSpec as P

SEQ = 8
TILES = 4
SPAN = 4
LAYERS = 2
LANES = 128
MESH = pl.DeviceIdType.MESH
BF16 = jnp.bfloat16
F32 = jnp.float32
INV_SQRT2 = float(np.sqrt(0.5))
INV_SQRT2PI = float(1.0 / np.sqrt(2.0 * np.pi))


def dot(left, right):
    return lax.dot_general(left, right, (((1,), (0,)), ((), ())), preferred_element_type=F32)


def dot_nt(left, right):
    return lax.dot_general(left, right, (((1,), (1,)), ((), ())), preferred_element_type=F32)


def gelu(x):
    return (0.5 * x) * (1.0 + lax.erf(x * INV_SQRT2))


def gelu_slope(x):
    return 0.5 * (1.0 + lax.erf(x * INV_SQRT2)) + x * (jnp.exp(-0.5 * x * x) * INV_SQRT2PI)


def rows_of(shape):
    return lax.broadcasted_iota(jnp.int32, shape, 0)


def cols_of(shape):
    return lax.broadcasted_iota(jnp.int32, shape, 1)


def one_hot(mask):
    return jnp.where(mask, 1.0, 0.0)


def eye(size):
    return one_hot(rows_of((size, size)) == cols_of((size, size))).astype(BF16)


def kernel(
    planes,
    texts,
    cuts,
    owner_ref,
    row_ref,
    border_ref,
    peer_ref,
    tokens_hbm,
    up_hbm,
    down_hbm,
    feat_hbm,
    near_hbm,
    tile_hbm,
    self_hbm,
    neigh_hbm,
    cot_hbm,
    node_out,
    text_out,
    down_out,
    tokens,
    up,
    down,
    feat,
    near,
    tile,
    self_w,
    neigh_w,
    cot,
    self_x,
    neigh_x,
    pool_x,
    h_full,
    agg_full,
    gz_full,
    edge_out,
    edge_in,
    back_out,
    back_in,
    a1_out,
    a1_in,
    a2_out,
    a2_in,
    r1_out,
    r1_in,
    r2_out,
    r2_in,
    tg_full,
    dp_out,
    dp_in,
    th_all,
    rs_out,
    rs_in,
    owner_keep,
    pool_keep,
    normed_keep,
    slope_keep,
    tile_w,
    tile_t,
    near_t,
    border_t,
    border_m,
    inv_keep,
    place,
    place_t,
    swap_m,
    swap_t,
    send_m,
    send_t,
    load_sem,
    up_sem,
    down_sem,
    wx_send,
    wx_recv,
    mp_send,
    mp_recv,
    edge_send,
    edge_recv,
    back_send,
    back_recv,
    all_send,
    all_recv,
    ring_send,
    ring_recv,
):
    dom = lax.axis_index("dom")
    core = lax.axis_index("mp")
    other = 1 - core
    domains = planes * a2_in.shape[0]
    spots = domains // planes
    z = dom // spots
    xy = lax.rem(dom, spots)
    half = feat.shape[1]
    nodes = feat.shape[0]
    bnd = edge_in.shape[2]
    pad = th_all.shape[1]
    sent_rows = -(-texts // 16) * 16

    loads = [
        pltpu.make_async_copy(src, dst, load_sem.at[i])
        for i, (src, dst) in enumerate(
            [
                (tokens_hbm, tokens),
                (feat_hbm, feat),
                (near_hbm, near),
                (tile_hbm, tile),
                (self_hbm, self_w),
                (neigh_hbm, neigh_w),
                (cot_hbm, cot),
            ]
        )
    ]
    chunks, _, chunk = up.shape
    up_loads = [
        pltpu.make_async_copy(up_hbm.at[:, pl.ds(c * chunk, chunk)], up.at[c], up_sem.at[c])
        for c in range(chunks)
    ]
    down_loads = [
        pltpu.make_async_copy(
            down_hbm.at[pl.ds(c * chunk, chunk), :],
            down.at[pl.ds(c * chunk, chunk), :],
            down_sem.at[c],
        )
        for c in range(chunks)
    ]
    loads[0].start()
    for c in range(chunks):
        up_loads[c].start()
        down_loads[c].start()
    for load in loads[1:]:
        load.start()

    barrier = pltpu.get_barrier_semaphore()

    def greet(device, mp):
        pl.semaphore_signal(barrier, inc=1, device_id=(device, mp), device_id_type=MESH)

    greet(dom, other)
    for i in range(1, planes):
        greet(lax.rem(z + i, planes) * spots + xy, core)
    for i in range(1, spots):
        greet(z * spots + lax.rem(xy + i, spots), core)
    for o in range(1, SPAN + 1):
        greet(lax.rem(dom + o, domains), core)
        greet(lax.rem(dom + domains - o, domains), core)

    up_steps, down_steps = planes // 2, (planes - 1) // 2
    ring_plan = [
        [(step, c) for step in range(steps) for c in range(chunks)] for steps in (up_steps, down_steps)
    ]
    ring_done = [0, 0]

    def ring(way, step, c):
        if way:
            block, to = lax.rem(z + step, planes), lax.rem(z + planes - 1, planes)
        else:
            block, to = lax.rem(z + planes - step, planes), lax.rem(z + 1, planes)
        view = th_all.at[block, pl.ds(0, sent_rows), pl.ds(c * chunk, chunk)]
        return pltpu.make_async_remote_copy(
            view,
            view,
            ring_send.at[way, step, c],
            ring_recv.at[way, step, c],
            device_id=(to * spots + xy, core),
            device_id_type=MESH,
        )

    def ring_arrive(way, step, c):
        if way:
            block = lax.rem(z + step + 1, planes)
        else:
            block = lax.rem(z + 2 * planes - step - 1, planes)
        view = th_all.at[block, pl.ds(0, sent_rows), pl.ds(c * chunk, chunk)]
        pltpu.make_async_copy(view, view, ring_recv.at[way, step, c]).wait()

    def ring_advance(way, count):
        for step, c in ring_plan[way][ring_done[way] : ring_done[way] + count]:
            if step > 0:
                ring_arrive(way, step - 1, c)
            ring(way, step, c).start()
            ring_done[way] += 1

    th_all[:, pl.ds(sent_rows, pad - sent_rows), :] = jnp.zeros(
        (planes, pad - sent_rows, th_all.shape[2]), BF16
    )
    rows = tokens.shape[0]
    mean_m = jnp.where(
        lax.shift_right_logical(cols_of((pad, rows)), 3) == rows_of((pad, rows)), 1.0 / SEQ, 0.0
    ).astype(BF16)
    loads[0].wait()
    for c in range(chunks):
        up_loads[c].wait()
        hidden = gelu(dot(tokens[...], up[c])).astype(BF16)
        mean_h = dot(mean_m, hidden).astype(BF16)
        th_all[z, :, pl.ds(c * chunk, chunk)] = mean_h
        down_loads[c].wait()
        partial = dot(mean_h, down[pl.ds(c * chunk, chunk), :])
        if c == 0:
            pool_keep[...] = partial
            pl.semaphore_wait(barrier, planes - 1 + spots - 1 + 2 * SPAN + 1)
        else:
            pool_keep[...] += partial
        ring_advance(0, 1)
        ring_advance(1, 1)

    def to_core(src, dst, slot):
        copy = pltpu.make_async_remote_copy(
            src, dst, mp_send.at[slot], mp_recv.at[slot], device_id=(dom, other), device_id_type=MESH
        )
        copy.start()
        return copy

    pool_copy = to_core(pool_keep.at[pl.ds(0, texts)], pool_x.at[pl.ds(0, texts)], 0)
    swaps = []
    for kind, (src, dst) in enumerate([(self_hbm, self_x), (neigh_hbm, neigh_x)]):
        for layer in range(LAYERS):
            copy = pltpu.make_async_remote_copy(
                src.at[layer, pl.ds(pl.multiple_of(other * half, half), half)],
                dst.at[layer],
                wx_send.at[kind, layer],
                wx_recv.at[kind, layer],
                device_id=(dom, other),
                device_id_type=MESH,
            )
            copy.start()
            swaps.append(copy)

    ring_advance(0, 1)
    ring_advance(1, 1)
    lines, lanes = owner_ref.shape
    line_of = rows_of((domains, lines)) * texts // lanes
    low = one_hot(cols_of((domains, lines)) == line_of).astype(BF16)
    high = one_hot(cols_of((domains, lines)) == line_of + 1).astype(BF16)
    shard = (domains, lanes)
    inside = cols_of(shard) + lax.rem(rows_of(shard) * texts, lanes) < lanes

    def by_shard(ref):
        flat = ref[...].astype(F32).astype(BF16)
        turned = [dot(m, flat) for m in (low, high)]
        for bit in range(lanes.bit_length() - 1):
            shift = (lanes - texts) * 2**bit % lanes
            if shift:
                moved = lax.rem(rows_of(shard) // 2**bit, 2) == 1
                turned = [jnp.where(moved, pltpu.roll(m, shift, 1), m) for m in turned]
        return jnp.where(cols_of(shard) < texts, jnp.where(inside, *turned), -1.0)

    owner_of = by_shard(owner_ref)
    row_of = by_shard(row_ref)
    owner_keep[...] = owner_of

    upper = one_hot(rows_of((pad, pad)) < cols_of((pad, pad))).astype(BF16)
    mine = owner_keep[pl.ds(dom, 1), :]
    named = one_hot(rows_of((domains, pad)).astype(F32) == mine)
    earlier = dot(named.astype(BF16), upper)
    first = jnp.where(earlier < 0.5, named, 0.0).reshape(planes, spots, pad)
    second = jnp.where(earlier > 0.5, named, 0.0).reshape(planes, spots, pad)
    send_m[...] = jnp.concatenate([first, second], axis=1).reshape(2 * domains, pad).astype(BF16)
    token_mean = dot(mean_m, tokens[...])

    pool_copy.wait_recv()
    in_text = rows_of((pad, 1)) < texts
    pooled = token_mean + pool_keep[...] + jnp.where(in_text, pool_x[...], 0.0)
    centre = pooled - jnp.mean(pooled, axis=-1, keepdims=True)
    inv_std = lax.rsqrt(jnp.mean(centre * centre, axis=-1, keepdims=True) + 1e-05)
    normed = centre * inv_std
    normed_keep[...] = normed
    own = jnp.where(core == 0, normed[:, :half], normed[:, half:]).astype(BF16)
    a1_out[...] = dot(send_m[...], own).astype(BF16).reshape(a1_out.shape)

    def part_of(ref, index, j):
        if j is None:
            return ref.at[index]
        return ref.at[index, :, pl.ds(*cuts[j])]

    def spread(src, dst, slot, j, count, me, device):
        sems = slot, j or 0
        for i in range(1, count):
            to = lax.rem(me + i, count)
            pltpu.make_async_remote_copy(
                part_of(src, to, j),
                part_of(dst, me, j),
                all_send.at[sems],
                all_recv.at[sems],
                device_id=(device(to), core),
                device_id_type=MESH,
            ).start()
        pltpu.make_async_copy(part_of(src, me, j), part_of(dst, me, j), all_recv.at[sems]).start()

    def spread_z(src, dst, slot, j=None):
        spread(src, dst, slot, j, planes, z, lambda to: to * spots + xy)

    def spread_xy(src, dst, slot, j=None):
        spread(src, dst, slot, j, spots, xy, lambda to: z * spots + to)

    def arrived(dst, slot, j=None):
        part = part_of(dst, pl.ds(0, dst.shape[0]), j)
        pltpu.make_async_copy(part, part, all_recv.at[slot, j or 0]).wait()

    def left(src, slot, j=None):
        part = part_of(src, pl.ds(0, src.shape[0] - 1), j)
        pltpu.make_async_copy(part, part, all_send.at[slot, j or 0]).wait()

    every = range(len(cuts))
    for j in every:
        spread_z(a1_out, a1_in, 0, j)

    mask = owner_of == dom.astype(F32)
    before = dot(one_hot(mask).astype(BF16), upper)
    row0 = jnp.max(jnp.where(mask & (before < 0.5), row_of, -1.0), axis=1, keepdims=True)
    row1 = jnp.max(jnp.where(mask & (before > 0.5), row_of, -1.0), axis=1, keepdims=True)
    node = cols_of((domains, nodes)).astype(F32)
    at0 = one_hot(node == row0).reshape(planes, spots, nodes)
    at1 = one_hot(node == row1).reshape(planes, spots, nodes)
    square = (2 * domains, 2 * domains)

    def swapped(index, inner, outer):
        low = lax.rem(index, inner)
        slot = lax.rem(index // inner, 2)
        high = index // (2 * inner)
        return low * (2 * outer) + slot * outer + high

    swap_m[...] = one_hot(cols_of(square) == swapped(rows_of(square), planes, spots)).astype(BF16)
    swap_t[...] = one_hot(cols_of(square) == swapped(rows_of(square), spots, planes)).astype(BF16)
    at = jnp.concatenate([at0, at1], axis=1).reshape(2 * domains, nodes).astype(BF16)
    place_t[...] = dot(swap_m[...], at).astype(BF16)
    place[...] = dot_nt(eye(nodes), place_t[...]).astype(BF16)
    send_t[...] = dot_nt(eye(pad), send_m[...]).astype(BF16)

    def rows_at(ref, j):
        return ref[:, :, pl.ds(*cuts[j])].reshape(-1, cuts[j][1])

    for j in every:
        arrived(a1_in, 0, j)
        moved = dot(swap_m[...], rows_at(a1_in, j)).astype(BF16)
        a2_out[:, :, pl.ds(*cuts[j])] = moved.reshape(spots, 2 * planes, -1)
        spread_xy(a2_out, a2_in, 1, j)
    ring_advance(0, 2)
    ring_advance(1, 2)

    for load in loads[1:]:
        load.wait()
    tall = tile.shape[0]
    for t in range(TILES):
        pick = one_hot(cols_of((nodes, tall)) == rows_of((nodes, tall)) * TILES + t).astype(BF16)
        tile_w[:, pl.ds(t * bnd, bnd)] = dot(pick, tile[...]).astype(BF16)
    for t in range(TILES):
        tile_t[pl.ds(t * bnd, bnd), :] = dot_nt(
            eye(bnd), tile_w[:, pl.ds(t * bnd, bnd)]
        ).astype(BF16)
    near_t[...] = dot_nt(eye(nodes), near[...]).astype(BF16)
    border = one_hot(rows_of((nodes, bnd)) == border_ref[...]).astype(BF16)
    for o in range(SPAN):
        border_m[:, pl.ds(o * bnd, bnd)] = border
    border_t[...] = dot_nt(eye(bnd), border).astype(BF16)
    degree = (
        1.0
        + dot(near[...], jnp.ones((nodes, half), BF16))
        + dot(tile_w[...], jnp.ones((TILES * bnd, half), BF16))
    )
    inv_keep[...] = 1.0 / degree

    own_k = pl.ds(pl.multiple_of(core * half, half), half)
    other_k = pl.ds(pl.multiple_of(other * half, half), half)

    def rows_in(which, j):
        start, size = cuts[j]
        return pl.ds(pl.multiple_of(which * half + start, math.gcd(half, start, size)), size)

    agg_slot = 1 + LAYERS
    gz_slot = agg_slot + LAYERS * len(cuts)
    tg_slot = gz_slot + LAYERS * len(cuts)
    core_copies, peer_copies = [pool_copy], []

    def share_cut(ref, index, slot, j):
        view = ref.at[(*index, core, slice(None), pl.ds(*cuts[j]))]
        core_copies.append(to_core(view, view, slot + j))

    def shared_cut(ref, index, slot, j):
        view = ref.at[(*index, other, slice(None), pl.ds(*cuts[j]))]
        pltpu.make_async_copy(view, view, mp_recv.at[slot + j]).wait()

    def to_partition(src, dst, send, recv, by):
        copy = pltpu.make_async_remote_copy(
            src,
            dst,
            send,
            recv,
            device_id=(lax.rem(dom + domains + by, domains), core),
            device_id_type=MESH,
        )
        copy.start()
        peer_copies.append(copy)
        return copy

    edge_copies = {}

    def emit_state(layer, j, state):
        at = pl.ds(*cuts[j])
        h_full[layer, core, :, at] = state
        edge_out[layer, :, at] = dot(border_t[...], state).astype(BF16)
        edge_copies[layer, j] = [
            to_partition(
                edge_out.at[layer, :, at],
                edge_in.at[layer, o, :, at],
                edge_send.at[layer, o, j],
                edge_recv.at[layer, o, j],
                o + 1,
            )
            for o in range(SPAN)
        ]

    def emit_gz(layer, j, grad):
        at = pl.ds(*cuts[j])
        gz_full[layer, core, :, at] = (grad * slope_keep[layer, :, at]).astype(BF16)
        share_cut(gz_full, (layer,), gz_slot + layer * len(cuts), j)

    for j in every:
        arrived(a2_in, 1, j)
        start = feat[:, pl.ds(*cuts[j])].astype(F32) + dot(place[...], rows_at(a2_in, j))
        emit_state(0, j, start.astype(BF16))

    for layer in range(LAYERS):
        own_h = h_full.at[layer, core]
        core_copies.append(to_core(own_h, own_h, 1 + layer))
        state = h_full[layer, core]
        total = state.astype(F32) + dot(near[...], state)
        pre = dot(state, self_w[layer, own_k, :])
        other_h = h_full.at[layer, other]
        pltpu.make_async_copy(other_h, other_h, mp_recv.at[1 + layer]).wait()
        pre += dot(h_full[layer, other], self_w[layer, other_k, :])
        ring_advance(0, 1)
        ring_advance(1, 2)
        for j in every:
            at = pl.ds(*cuts[j])
            for copy in edge_copies[layer, j]:
                copy.wait_recv()
            here = total[:, cuts[j][0] : sum(cuts[j])]
            for t in range(TILES):
                picked = edge_in[layer, 0, :, at]
                for o in range(1, SPAN):
                    picked = jnp.where(peer_ref[0, t] == o, edge_in[layer, o, :, at], picked)
                here += dot(tile_w[:, pl.ds(t * bnd, bnd)], picked)
            agg = (here * inv_keep[:, at]).astype(BF16)
            agg_full[layer, core, :, at] = agg
            share_cut(agg_full, (layer,), agg_slot + layer * len(cuts), j)
            pre += dot(agg, neigh_w[layer, rows_in(core, j), :])
        for j in every:
            shared_cut(agg_full, (layer,), agg_slot + layer * len(cuts), j)
            if j < len(cuts) - 1:
                pre += dot(agg_full[layer, other, :, pl.ds(*cuts[j])], neigh_w[layer, rows_in(other, j), :])
        last = agg_full[layer, other, :, pl.ds(*cuts[-1])]
        kept = []
        for j in every:
            at = pl.ds(*cuts[j])
            done = pre[:, cuts[j][0] : sum(cuts[j])] + dot(
                last, neigh_w[layer, rows_in(other, len(cuts) - 1), at]
            )
            if layer < LAYERS - 1:
                emit_state(layer + 1, j, gelu(done).astype(BF16))
            else:
                slope_keep[layer, :, at] = gelu_slope(done)
                emit_gz(layer, j, cot[:, at].astype(F32))
            kept.append(done)
        for j in every:
            at = pl.ds(*cuts[j])
            if layer < LAYERS - 1:
                slope_keep[layer, :, at] = gelu_slope(kept[j])
            else:
                node_out[:, at] = gelu(kept[j]).astype(BF16)

    for copy in swaps:
        copy.wait()
    for layer in reversed(range(LAYERS)):
        gz = gz_full[layer, core]
        self_part = dot_nt(gz, self_w[layer, own_k, :])
        mean_part = dot_nt(gz, neigh_w[layer, own_k, :])
        for j in every:
            shared_cut(gz_full, (layer,), gz_slot + layer * len(cuts), j)
        gz = gz_full[layer, other]
        back_copies, scaled = [], []
        for j in every:
            at = pl.ds(*cuts[j])
            mean = mean_part[:, cuts[j][0] : sum(cuts[j])] + dot_nt(gz, neigh_x[layer, at, :])
            scaled.append((mean * inv_keep[:, at]).astype(BF16))
            pieces = [dot(tile_t[pl.ds(t * bnd, bnd), :], scaled[j]) for t in range(TILES)]
            sent = []
            for o in range(SPAN):
                bundle = jnp.where(peer_ref[0, 0] == o, pieces[0], 0.0)
                for t in range(1, TILES):
                    bundle += jnp.where(peer_ref[0, t] == o, pieces[t], 0.0)
                back_out[layer, o, :, at] = bundle.astype(BF16)
                sent.append(
                    to_partition(
                        back_out.at[layer, o, :, at],
                        back_in.at[layer, o, :, at],
                        back_send.at[layer, o, j],
                        back_recv.at[layer, o, j],
                        -(o + 1),
                    )
                )
            back_copies.append(sent)
        self_part += dot_nt(gz, self_x[layer])
        grads = [
            self_part[:, cuts[j][0] : sum(cuts[j])]
            + scaled[j].astype(F32)
            + dot(near_t[...], scaled[j])
            for j in every
        ]
        ring_advance(0, 2)
        for j in every:
            at = pl.ds(*cuts[j])
            for copy in back_copies[j]:
                copy.wait_recv()
            grad = grads[j] + dot(
                border_m[...], back_in[layer, :, :, at].reshape(SPAN * bnd, cuts[j][1])
            )
            if layer > 0:
                emit_gz(layer - 1, j, grad)
            else:
                back = dot(place_t[...], grad.astype(BF16)).astype(BF16)
                r1_out[:, :, at] = back.reshape(spots, 2 * planes, -1)
                spread_xy(r1_out, r1_in, 2, j)

    ring_advance(0, len(ring_plan[0]))
    ring_advance(1, len(ring_plan[1]))
    for j in every:
        arrived(r1_in, 2, j)
        moved = dot(swap_t[...], rows_at(r1_in, j)).astype(BF16)
        r2_out[:, :, pl.ds(*cuts[j])] = moved.reshape(planes, 2 * spots, -1)
        spread_z(r2_out, r2_in, 3, j)
    for j in every:
        at = pl.ds(*cuts[j])
        arrived(r2_in, 3, j)
        text_grad = dot(send_t[...], rows_at(r2_in, j))
        tg_full[core, :, at] = text_grad.astype(BF16)
        share_cut(tg_full, (), tg_slot, j)
        text_out[:, at] = text_grad[:texts]
    for j in every:
        shared_cut(tg_full, (), tg_slot, j)
    full = jnp.concatenate([tg_full[0], tg_full[1]], axis=1).astype(F32)
    normed = normed_keep[...]
    mean_grad = jnp.mean(full, axis=-1, keepdims=True)
    mean_cross = jnp.mean(full * normed, axis=-1, keepdims=True)
    dpooled = inv_std * (full - mean_grad - normed * mean_cross)
    dp_out[...] = dpooled.T.astype(BF16).reshape(dp_out.shape)
    spread_z(dp_out, dp_in, 4)

    slab = dp_in.shape[1]
    share = slab // spots
    room = rs_in.shape[1] // 2
    spread_shape = (spots * room, slab)
    row_at = lax.rem(rows_of(spread_shape), room)
    pick = one_hot(
        (row_at < share) & (cols_of(spread_shape) == rows_of(spread_shape) // room * share + row_at)
    ).astype(BF16)
    arrived(dp_in, 4)
    for way, steps in ((0, up_steps), (1, down_steps)):
        for c in range(chunks if steps else 0):
            ring_arrive(way, steps - 1, c)
    joined = jnp.concatenate([dp_in[i] for i in range(planes)], axis=1)
    joined = dot(pick, joined).astype(BF16)
    means = th_all[...].reshape(planes * pad, th_all.shape[2])
    part = dot(joined, means)
    cut = part.shape[1] // 2
    rs_out[...] = jnp.concatenate(
        [part[:, :cut].reshape(spots, room, cut), part[:, cut:].reshape(spots, room, cut)], axis=1
    ).astype(BF16)
    spread_xy(rs_out, rs_in, 5)
    arrived(rs_in, 5)
    total = jnp.sum(rs_in[...].astype(F32), axis=0)
    down_out[:, pl.ds(0, cut)] = total[:share]
    down_out[:, pl.ds(cut, cut)] = total[room : room + share]

    for copy in core_copies + peer_copies:
        copy.wait_send()
    for slot, src in enumerate((a1_out, a2_out, r1_out, r2_out)):
        for j in every:
            left(src, slot, j)
    left(dp_out, 4)
    left(rs_out, 5)
    for way in (0, 1):
        for step, c in ring_plan[way]:
            ring(way, step, c).wait_send()


def finish(node_ref, text_ref, down_ref, node_out, text_out, down_out):
    node_out[...] = node_ref[...]
    text_out[...] = text_ref[...]
    down_out[...] = down_ref[...]


def column_cuts(half):
    first = LANES if half > LANES else half // 2
    return ((0, first), (first, half - first))


def local(
    tokens,
    up_weight,
    down_weight,
    text_owner,
    text_row,
    node_feat,
    local_weight,
    tile_weight,
    tile_peer,
    boundary_rows,
    self_weight,
    neigh_weight,
    node_cot,
    planes,
):
    domains = lax.axis_size("dom")
    spots = domains // planes
    rows, width = tokens.shape
    texts = rows // SEQ
    pad = -(-texts // LANES) * LANES
    nodes, half = node_feat.shape
    bnd = boundary_rows.shape[1]
    hidden = up_weight.shape[1]
    chunk = min(512, hidden)
    chunks = hidden // chunk
    cuts = column_cuts(half)
    core_slots = 1 + LAYERS + (2 * LAYERS + 1) * len(cuts)
    share = width // domains
    room = -(-share // 8) * 8
    slab = width // planes

    owners = text_owner.reshape(-1, LANES)
    text_rows = text_row.reshape(-1, LANES)
    tile = tile_weight.reshape(nodes * TILES, bnd)

    def vm(*shape, dtype=BF16):
        return pltpu.VMEM(shape, dtype)

    dma = pltpu.SemaphoreType.DMA
    scratch = [
        vm(rows, width),
        vm(chunks, width, chunk),
        vm(hidden, width),
        vm(nodes, half),
        vm(nodes, nodes),
        vm(nodes * TILES, bnd),
        vm(LAYERS, width, half),
        vm(LAYERS, width, half),
        vm(nodes, half),
        vm(LAYERS, half, half),
        vm(LAYERS, half, half),
        vm(pad, width, dtype=F32),
        vm(LAYERS, 2, nodes, half),
        vm(LAYERS, 2, nodes, half),
        vm(LAYERS, 2, nodes, half),
        vm(LAYERS, bnd, half),
        vm(LAYERS, SPAN, bnd, half),
        vm(LAYERS, SPAN, bnd, half),
        vm(LAYERS, SPAN, bnd, half),
        vm(planes, 2 * spots, half),
        vm(planes, 2 * spots, half),
        vm(spots, 2 * planes, half),
        vm(spots, 2 * planes, half),
        vm(spots, 2 * planes, half),
        vm(spots, 2 * planes, half),
        vm(planes, 2 * spots, half),
        vm(planes, 2 * spots, half),
        vm(2, pad, half),
        vm(planes, slab, pad),
        vm(planes, slab, pad),
        vm(planes, pad, hidden),
        vm(spots, 2 * room, hidden // 2),
        vm(spots, 2 * room, hidden // 2),
        vm(domains, LANES, dtype=F32),
        vm(pad, width, dtype=F32),
        vm(pad, width, dtype=F32),
        vm(LAYERS, nodes, half, dtype=F32),
        vm(nodes, TILES * bnd),
        vm(TILES * bnd, nodes),
        vm(nodes, nodes),
        vm(bnd, nodes),
        vm(nodes, SPAN * bnd),
        vm(nodes, half, dtype=F32),
        vm(nodes, 2 * domains),
        vm(2 * domains, nodes),
        vm(2 * domains, 2 * domains),
        vm(2 * domains, 2 * domains),
        vm(2 * domains, pad),
        vm(pad, 2 * domains),
        dma((7,)),
        dma((chunks,)),
        dma((chunks,)),
        dma((2, LAYERS)),
        dma((2, LAYERS)),
        dma((core_slots,)),
        dma((core_slots,)),
        dma((LAYERS, SPAN, len(cuts))),
        dma((LAYERS, SPAN, len(cuts))),
        dma((LAYERS, SPAN, len(cuts))),
        dma((LAYERS, SPAN, len(cuts))),
        dma((6, len(cuts))),
        dma((6, len(cuts))),
        dma((2, max(1, planes // 2), chunks)),
        dma((2, max(1, planes // 2), chunks)),
    ]
    vmem = pl.BlockSpec(memory_space=pltpu.VMEM)
    smem = pl.BlockSpec(memory_space=pltpu.SMEM)
    hbm = pl.BlockSpec(memory_space=pl.ANY)
    out_shape = (
        jax.ShapeDtypeStruct((nodes, half), BF16),
        jax.ShapeDtypeStruct((texts, half), F32),
        jax.ShapeDtypeStruct((share, hidden), F32),
    )
    results = pl.pallas_call(
        functools.partial(kernel, planes, texts, cuts),
        out_shape=out_shape,
        in_specs=[vmem, vmem, vmem, smem] + [hbm] * 9,
        out_specs=(vmem, vmem, vmem),
        scratch_shapes=scratch,
        compiler_params=pltpu.CompilerParams(
            collective_id=0, has_side_effects=True, vmem_limit_bytes=58 * 2**20
        ),
    )(
        owners,
        text_rows,
        boundary_rows,
        tile_peer,
        tokens,
        up_weight,
        down_weight,
        node_feat,
        local_weight,
        tile,
        self_weight,
        neigh_weight,
        node_cot,
    )
    return pl.pallas_call(
        finish,
        out_shape=out_shape,
        in_specs=[vmem] * 3,
        out_specs=(vmem,) * 3,
    )(*results)


def solution(mesh):
    in_specs = (
        P("dom", None),
        P(None, "mp"),
        P("mp", None),
        P(),
        P(),
        P("dom", "mp"),
        P("dom", None),
        P("dom", None, None),
        P("dom", None),
        P("dom", None),
        P(None, None, "mp"),
        P(None, None, "mp"),
        P("dom", "mp"),
    )
    out_specs = (P("dom", "mp"), P("dom", "mp"), P("dom", "mp"))
    domains = mesh.shape["dom"]
    planes = 8 if domains >= 128 else 2
    return jax.shard_map(
        functools.partial(local, planes=planes),
        mesh=mesh,
        in_specs=in_specs,
        out_specs=out_specs,
        check_vma=False,
    )
```

```python
import functools
import math

import jax
import jax.numpy as jnp
import numpy as np
from jax import lax
from jax.experimental import pallas as pl
from jax.experimental.pallas import tpu as pltpu
from jax.sharding import PartitionSpec as P

SEQ = 8
TILES = 4
SPAN = 4
LAYERS = 2
LANES = 128
MESH = pl.DeviceIdType.MESH
BF16 = jnp.bfloat16
F32 = jnp.float32
INV_SQRT2 = float(np.sqrt(0.5))
INV_SQRT2PI = float(1.0 / np.sqrt(2.0 * np.pi))


def dot(left, right):
    return lax.dot_general(left, right, (((1,), (0,)), ((), ())), preferred_element_type=F32)


def dot_nt(left, right):
    return lax.dot_general(left, right, (((1,), (1,)), ((), ())), preferred_element_type=F32)


def gelu(x):
    return (0.5 * x) * (1.0 + lax.erf(x * INV_SQRT2))


def gelu_slope(x):
    return 0.5 * (1.0 + lax.erf(x * INV_SQRT2)) + x * (jnp.exp(-0.5 * x * x) * INV_SQRT2PI)


def rows_of(shape):
    return lax.broadcasted_iota(jnp.int32, shape, 0)


def cols_of(shape):
    return lax.broadcasted_iota(jnp.int32, shape, 1)


def one_hot(mask):
    return jnp.where(mask, 1.0, 0.0)


def eye(size):
    return one_hot(rows_of((size, size)) == cols_of((size, size))).astype(BF16)


def kernel(
    planes,
    texts,
    cuts,
    owner_ref,
    row_ref,
    border_ref,
    peer_ref,
    tokens_hbm,
    up_hbm,
    down_hbm,
    feat_hbm,
    near_hbm,
    tile_hbm,
    self_hbm,
    neigh_hbm,
    cot_hbm,
    node_out,
    text_out,
    down_out,
    tokens,
    up,
    down,
    feat,
    near,
    tile,
    self_w,
    neigh_w,
    cot,
    self_x,
    neigh_x,
    pool_x,
    h_full,
    agg_full,
    gz_full,
    edge_out,
    edge_in,
    back_out,
    back_in,
    a1_out,
    a1_in,
    a2_out,
    a2_in,
    r1_out,
    r1_in,
    r2_out,
    r2_in,
    tg_full,
    dp_out,
    dp_in,
    th_all,
    rs_out,
    rs_in,
    owner_keep,
    pool_keep,
    normed_keep,
    slope_keep,
    tile_w,
    tile_t,
    near_t,
    border_t,
    border_m,
    inv_keep,
    place,
    place_t,
    swap_m,
    swap_t,
    send_m,
    send_t,
    load_sem,
    up_sem,
    down_sem,
    wx_send,
    wx_recv,
    mp_send,
    mp_recv,
    edge_send,
    edge_recv,
    back_send,
    back_recv,
    all_send,
    all_recv,
    ring_send,
    ring_recv,
):
    dom = lax.axis_index("dom")
    core = lax.axis_index("mp")
    other = 1 - core
    domains = planes * a2_in.shape[0]
    spots = domains // planes
    z = dom // spots
    xy = lax.rem(dom, spots)
    half = feat.shape[1]
    nodes = feat.shape[0]
    bnd = edge_in.shape[2]
    pad = th_all.shape[1]
    sent_rows = -(-texts // 16) * 16

    loads = [
        pltpu.make_async_copy(src, dst, load_sem.at[i])
        for i, (src, dst) in enumerate(
            [
                (tokens_hbm, tokens),
                (feat_hbm, feat),
                (near_hbm, near),
                (tile_hbm, tile),
                (self_hbm, self_w),
                (neigh_hbm, neigh_w),
                (cot_hbm, cot),
            ]
        )
    ]
    chunks, _, chunk = up.shape
    up_loads = [
        pltpu.make_async_copy(up_hbm.at[:, pl.ds(c * chunk, chunk)], up.at[c], up_sem.at[c])
        for c in range(chunks)
    ]
    down_loads = [
        pltpu.make_async_copy(
            down_hbm.at[pl.ds(c * chunk, chunk), :],
            down.at[pl.ds(c * chunk, chunk), :],
            down_sem.at[c],
        )
        for c in range(chunks)
    ]
    loads[0].start()
    for c in range(chunks):
        up_loads[c].start()
        down_loads[c].start()
    for load in loads[1:]:
        load.start()

    barrier = pltpu.get_barrier_semaphore()

    def greet(device, mp):
        pl.semaphore_signal(barrier, inc=1, device_id=(device, mp), device_id_type=MESH)

    greet(dom, other)
    for i in range(1, planes):
        greet(lax.rem(z + i, planes) * spots + xy, core)
    for i in range(1, spots):
        greet(z * spots + lax.rem(xy + i, spots), core)
    for o in range(1, SPAN + 1):
        greet(lax.rem(dom + o, domains), core)
        greet(lax.rem(dom + domains - o, domains), core)

    up_steps, down_steps = planes // 2, (planes - 1) // 2
    ring_plan = [
        [(step, c) for step in range(steps) for c in range(chunks)] for steps in (up_steps, down_steps)
    ]
    ring_done = [0, 0]

    def ring(way, step, c):
        if way:
            block, to = lax.rem(z + step, planes), lax.rem(z + planes - 1, planes)
        else:
            block, to = lax.rem(z + planes - step, planes), lax.rem(z + 1, planes)
        view = th_all.at[block, pl.ds(0, sent_rows), pl.ds(c * chunk, chunk)]
        return pltpu.make_async_remote_copy(
            view,
            view,
            ring_send.at[way, step, c],
            ring_recv.at[way, step, c],
            device_id=(to * spots + xy, core),
            device_id_type=MESH,
        )

    def ring_arrive(way, step, c):
        if way:
            block = lax.rem(z + step + 1, planes)
        else:
            block = lax.rem(z + 2 * planes - step - 1, planes)
        view = th_all.at[block, pl.ds(0, sent_rows), pl.ds(c * chunk, chunk)]
        pltpu.make_async_copy(view, view, ring_recv.at[way, step, c]).wait()

    def ring_advance(way, count):
        for step, c in ring_plan[way][ring_done[way] : ring_done[way] + count]:
            if step > 0:
                ring_arrive(way, step - 1, c)
            ring(way, step, c).start()
            ring_done[way] += 1

    swaps = []

    def swap_weights():
        for kind, (src, dst) in enumerate([(self_hbm, self_x), (neigh_hbm, neigh_x)]):
            for layer in range(LAYERS):
                copy = pltpu.make_async_remote_copy(
                    src.at[layer, pl.ds(pl.multiple_of(other * half, half), half)],
                    dst.at[layer],
                    wx_send.at[kind, layer],
                    wx_recv.at[kind, layer],
                    device_id=(dom, other),
                    device_id_type=MESH,
                )
                copy.start()
                swaps.append(copy)

    th_all[:, pl.ds(sent_rows, pad - sent_rows), :] = jnp.zeros(
        (planes, pad - sent_rows, th_all.shape[2]), BF16
    )
    rows = tokens.shape[0]
    mean_m = jnp.where(
        lax.shift_right_logical(cols_of((pad, rows)), 3) == rows_of((pad, rows)), 1.0 / SEQ, 0.0
    ).astype(BF16)
    loads[0].wait()
    for c in range(chunks):
        up_loads[c].wait()
        hidden = gelu(dot(tokens[...], up[c])).astype(BF16)
        mean_h = dot(mean_m, hidden).astype(BF16)
        th_all[z, :, pl.ds(c * chunk, chunk)] = mean_h
        down_loads[c].wait()
        partial = dot(mean_h, down[pl.ds(c * chunk, chunk), :])
        if c == 0:
            pool_keep[...] = partial
            pl.semaphore_wait(barrier, planes - 1 + spots - 1 + 2 * SPAN + 1)
            swap_weights()
        else:
            pool_keep[...] += partial
        ring_advance(0, 1)
        ring_advance(1, 1)

    def to_core(src, dst, slot):
        copy = pltpu.make_async_remote_copy(
            src, dst, mp_send.at[slot], mp_recv.at[slot], device_id=(dom, other), device_id_type=MESH
        )
        copy.start()
        return copy

    pool_copy = to_core(pool_keep.at[pl.ds(0, texts)], pool_x.at[pl.ds(0, texts)], 0)
    lines, lanes = owner_ref.shape
    line_of = rows_of((domains, lines)) * texts // lanes
    low = one_hot(cols_of((domains, lines)) == line_of).astype(BF16)
    high = one_hot(cols_of((domains, lines)) == line_of + 1).astype(BF16)
    shard = (domains, lanes)
    inside = cols_of(shard) + lax.rem(rows_of(shard) * texts, lanes) < lanes

    def by_shard(ref):
        flat = ref[...].astype(F32).astype(BF16)
        turned = [dot(m, flat) for m in (low, high)]
        for bit in range(lanes.bit_length() - 1):
            shift = (lanes - texts) * 2**bit % lanes
            if shift:
                moved = lax.rem(rows_of(shard) // 2**bit, 2) == 1
                turned = [jnp.where(moved, pltpu.roll(m, shift, 1), m) for m in turned]
        return jnp.where(cols_of(shard) < texts, jnp.where(inside, *turned), -1.0)

    owner_of = by_shard(owner_ref)
    row_of = by_shard(row_ref)
    owner_keep[...] = owner_of

    upper = one_hot(rows_of((pad, pad)) < cols_of((pad, pad))).astype(BF16)
    mine = owner_keep[pl.ds(dom, 1), :]
    named = one_hot(rows_of((domains, pad)).astype(F32) == mine)
    earlier = dot(named.astype(BF16), upper)
    first = jnp.where(earlier < 0.5, named, 0.0).reshape(planes, spots, pad)
    second = jnp.where(earlier > 0.5, named, 0.0).reshape(planes, spots, pad)
    send_m[...] = jnp.concatenate([first, second], axis=1).reshape(2 * domains, pad).astype(BF16)
    token_mean = dot(mean_m, tokens[...])

    pool_copy.wait_recv()
    in_text = rows_of((pad, 1)) < texts
    pooled = token_mean + pool_keep[...] + jnp.where(in_text, pool_x[...], 0.0)
    centre = pooled - jnp.mean(pooled, axis=-1, keepdims=True)
    inv_std = lax.rsqrt(jnp.mean(centre * centre, axis=-1, keepdims=True) + 1e-05)
    normed = centre * inv_std
    normed_keep[...] = normed
    own = jnp.where(core == 0, normed[:, :half], normed[:, half:]).astype(BF16)
    a1_out[...] = dot(send_m[...], own).astype(BF16).reshape(a1_out.shape)

    def part_of(ref, index, j):
        if j is None:
            return ref.at[index]
        return ref.at[index, :, pl.ds(*cuts[j])]

    def spread(src, dst, slot, j, count, me, device):
        sems = slot, j or 0
        for i in range(1, count):
            to = lax.rem(me + i, count)
            pltpu.make_async_remote_copy(
                part_of(src, to, j),
                part_of(dst, me, j),
                all_send.at[sems],
                all_recv.at[sems],
                device_id=(device(to), core),
                device_id_type=MESH,
            ).start()
        pltpu.make_async_copy(part_of(src, me, j), part_of(dst, me, j), all_recv.at[sems]).start()

    def spread_z(src, dst, slot, j=None):
        spread(src, dst, slot, j, planes, z, lambda to: to * spots + xy)

    def spread_xy(src, dst, slot, j=None):
        spread(src, dst, slot, j, spots, xy, lambda to: z * spots + to)

    def arrived(dst, slot, j=None):
        part = part_of(dst, pl.ds(0, dst.shape[0]), j)
        pltpu.make_async_copy(part, part, all_recv.at[slot, j or 0]).wait()

    def left(src, slot, j=None):
        part = part_of(src, pl.ds(0, src.shape[0] - 1), j)
        pltpu.make_async_copy(part, part, all_send.at[slot, j or 0]).wait()

    every = range(len(cuts))
    for j in every:
        spread_z(a1_out, a1_in, 0, j)

    mask = owner_of == dom.astype(F32)
    before = dot(one_hot(mask).astype(BF16), upper)
    row0 = jnp.max(jnp.where(mask & (before < 0.5), row_of, -1.0), axis=1, keepdims=True)
    row1 = jnp.max(jnp.where(mask & (before > 0.5), row_of, -1.0), axis=1, keepdims=True)
    node = cols_of((domains, nodes)).astype(F32)
    at0 = one_hot(node == row0).reshape(planes, spots, nodes)
    at1 = one_hot(node == row1).reshape(planes, spots, nodes)
    square = (2 * domains, 2 * domains)

    def swapped(index, inner, outer):
        low = lax.rem(index, inner)
        slot = lax.rem(index // inner, 2)
        high = index // (2 * inner)
        return low * (2 * outer) + slot * outer + high

    swap_m[...] = one_hot(cols_of(square) == swapped(rows_of(square), planes, spots)).astype(BF16)
    swap_t[...] = one_hot(cols_of(square) == swapped(rows_of(square), spots, planes)).astype(BF16)
    at = jnp.concatenate([at0, at1], axis=1).reshape(2 * domains, nodes).astype(BF16)
    place_t[...] = dot(swap_m[...], at).astype(BF16)
    place[...] = dot_nt(eye(nodes), place_t[...]).astype(BF16)
    send_t[...] = dot_nt(eye(pad), send_m[...]).astype(BF16)

    def rows_at(ref, j):
        return ref[:, :, pl.ds(*cuts[j])].reshape(-1, cuts[j][1])

    for j in every:
        arrived(a1_in, 0, j)
        moved = dot(swap_m[...], rows_at(a1_in, j)).astype(BF16)
        a2_out[:, :, pl.ds(*cuts[j])] = moved.reshape(spots, 2 * planes, -1)
        spread_xy(a2_out, a2_in, 1, j)
    ring_advance(0, 2)
    ring_advance(1, 2)

    for load in loads[1:]:
        load.wait()
    tall = tile.shape[0]
    for t in range(TILES):
        pick = one_hot(cols_of((nodes, tall)) == rows_of((nodes, tall)) * TILES + t).astype(BF16)
        tile_w[:, pl.ds(t * bnd, bnd)] = dot(pick, tile[...]).astype(BF16)
    for t in range(TILES):
        tile_t[pl.ds(t * bnd, bnd), :] = dot_nt(
            eye(bnd), tile_w[:, pl.ds(t * bnd, bnd)]
        ).astype(BF16)
    near_t[...] = dot_nt(eye(nodes), near[...]).astype(BF16)
    border = one_hot(rows_of((nodes, bnd)) == border_ref[...]).astype(BF16)
    for o in range(SPAN):
        border_m[:, pl.ds(o * bnd, bnd)] = border
    border_t[...] = dot_nt(eye(bnd), border).astype(BF16)
    degree = (
        1.0
        + dot(near[...], jnp.ones((nodes, half), BF16))
        + dot(tile_w[...], jnp.ones((TILES * bnd, half), BF16))
    )
    inv_keep[...] = 1.0 / degree

    own_k = pl.ds(pl.multiple_of(core * half, half), half)
    other_k = pl.ds(pl.multiple_of(other * half, half), half)

    def rows_in(which, j):
        start, size = cuts[j]
        return pl.ds(pl.multiple_of(which * half + start, math.gcd(half, start, size)), size)

    agg_slot = 1 + LAYERS
    gz_slot = agg_slot + LAYERS * len(cuts)
    tg_slot = gz_slot + LAYERS * len(cuts)
    core_copies, peer_copies = [pool_copy], []

    def share_cut(ref, index, slot, j):
        view = ref.at[(*index, core, slice(None), pl.ds(*cuts[j]))]
        core_copies.append(to_core(view, view, slot + j))

    def shared_cut(ref, index, slot, j):
        view = ref.at[(*index, other, slice(None), pl.ds(*cuts[j]))]
        pltpu.make_async_copy(view, view, mp_recv.at[slot + j]).wait()

    def to_partition(src, dst, send, recv, by):
        copy = pltpu.make_async_remote_copy(
            src,
            dst,
            send,
            recv,
            device_id=(lax.rem(dom + domains + by, domains), core),
            device_id_type=MESH,
        )
        copy.start()
        peer_copies.append(copy)
        return copy

    edge_copies = {}

    def emit_state(layer, j, state):
        at = pl.ds(*cuts[j])
        h_full[layer, core, :, at] = state
        edge_out[layer, :, at] = dot(border_t[...], state).astype(BF16)
        edge_copies[layer, j] = [
            to_partition(
                edge_out.at[layer, :, at],
                edge_in.at[layer, o, :, at],
                edge_send.at[layer, o, j],
                edge_recv.at[layer, o, j],
                o + 1,
            )
            for o in range(SPAN)
        ]

    def emit_gz(layer, j, grad):
        at = pl.ds(*cuts[j])
        gz_full[layer, core, :, at] = (grad * slope_keep[layer, :, at]).astype(BF16)
        share_cut(gz_full, (layer,), gz_slot + layer * len(cuts), j)

    for j in every:
        arrived(a2_in, 1, j)
        start = feat[:, pl.ds(*cuts[j])].astype(F32) + dot(place[...], rows_at(a2_in, j))
        emit_state(0, j, start.astype(BF16))

    for layer in range(LAYERS):
        own_h = h_full.at[layer, core]
        core_copies.append(to_core(own_h, own_h, 1 + layer))
        state = h_full[layer, core]
        total = state.astype(F32) + dot(near[...], state)
        pre = dot(state, self_w[layer, own_k, :])
        other_h = h_full.at[layer, other]
        pltpu.make_async_copy(other_h, other_h, mp_recv.at[1 + layer]).wait()
        pre += dot(h_full[layer, other], self_w[layer, other_k, :])
        ring_advance(0, 1 + layer)
        ring_advance(1, 2)
        for j in every:
            at = pl.ds(*cuts[j])
            for copy in edge_copies[layer, j]:
                copy.wait_recv()
            here = total[:, cuts[j][0] : sum(cuts[j])]
            for t in range(TILES):
                picked = edge_in[layer, 0, :, at]
                for o in range(1, SPAN):
                    picked = jnp.where(peer_ref[0, t] == o, edge_in[layer, o, :, at], picked)
                here += dot(tile_w[:, pl.ds(t * bnd, bnd)], picked)
            agg = (here * inv_keep[:, at]).astype(BF16)
            agg_full[layer, core, :, at] = agg
            share_cut(agg_full, (layer,), agg_slot + layer * len(cuts), j)
            pre += dot(agg, neigh_w[layer, rows_in(core, j), :])
        for j in every:
            shared_cut(agg_full, (layer,), agg_slot + layer * len(cuts), j)
            if j < len(cuts) - 1:
                pre += dot(agg_full[layer, other, :, pl.ds(*cuts[j])], neigh_w[layer, rows_in(other, j), :])
        last = agg_full[layer, other, :, pl.ds(*cuts[-1])]
        kept = []
        for j in every:
            at = pl.ds(*cuts[j])
            done = pre[:, cuts[j][0] : sum(cuts[j])] + dot(
                last, neigh_w[layer, rows_in(other, len(cuts) - 1), at]
            )
            if layer < LAYERS - 1:
                emit_state(layer + 1, j, gelu(done).astype(BF16))
            else:
                slope_keep[layer, :, at] = gelu_slope(done)
                emit_gz(layer, j, cot[:, at].astype(F32))
            kept.append(done)
        for j in every:
            at = pl.ds(*cuts[j])
            if layer < LAYERS - 1:
                slope_keep[layer, :, at] = gelu_slope(kept[j])
            else:
                node_out[:, at] = gelu(kept[j]).astype(BF16)

    for copy in swaps:
        copy.wait()
    for layer in reversed(range(LAYERS)):
        gz = gz_full[layer, core]
        self_part = dot_nt(gz, self_w[layer, own_k, :])
        mean_part = dot_nt(gz, neigh_w[layer, own_k, :])
        for j in every:
            shared_cut(gz_full, (layer,), gz_slot + layer * len(cuts), j)
        gz = gz_full[layer, other]
        back_copies, scaled = [], []
        for j in every:
            at = pl.ds(*cuts[j])
            mean = mean_part[:, cuts[j][0] : sum(cuts[j])] + dot_nt(gz, neigh_x[layer, at, :])
            scaled.append((mean * inv_keep[:, at]).astype(BF16))
            pieces = [dot(tile_t[pl.ds(t * bnd, bnd), :], scaled[j]) for t in range(TILES)]
            sent = []
            for o in range(SPAN):
                bundle = jnp.where(peer_ref[0, 0] == o, pieces[0], 0.0)
                for t in range(1, TILES):
                    bundle += jnp.where(peer_ref[0, t] == o, pieces[t], 0.0)
                back_out[layer, o, :, at] = bundle.astype(BF16)
                sent.append(
                    to_partition(
                        back_out.at[layer, o, :, at],
                        back_in.at[layer, o, :, at],
                        back_send.at[layer, o, j],
                        back_recv.at[layer, o, j],
                        -(o + 1),
                    )
                )
            back_copies.append(sent)
        self_part += dot_nt(gz, self_x[layer])
        grads = [
            self_part[:, cuts[j][0] : sum(cuts[j])]
            + scaled[j].astype(F32)
            + dot(near_t[...], scaled[j])
            for j in every
        ]
        ring_advance(0, 2)
        for j in every:
            at = pl.ds(*cuts[j])
            for copy in back_copies[j]:
                copy.wait_recv()
            grad = grads[j] + dot(
                border_m[...], back_in[layer, :, :, at].reshape(SPAN * bnd, cuts[j][1])
            )
            if layer > 0:
                emit_gz(layer - 1, j, grad)
            else:
                back = dot(place_t[...], grad.astype(BF16)).astype(BF16)
                r1_out[:, :, at] = back.reshape(spots, 2 * planes, -1)
                spread_xy(r1_out, r1_in, 2, j)

    ring_advance(0, len(ring_plan[0]))
    ring_advance(1, len(ring_plan[1]))
    for j in every:
        arrived(r1_in, 2, j)
        moved = dot(swap_t[...], rows_at(r1_in, j)).astype(BF16)
        r2_out[:, :, pl.ds(*cuts[j])] = moved.reshape(planes, 2 * spots, -1)
        spread_z(r2_out, r2_in, 3, j)
    for j in every:
        at = pl.ds(*cuts[j])
        arrived(r2_in, 3, j)
        text_grad = dot(send_t[...], rows_at(r2_in, j))
        tg_full[core, :, at] = text_grad.astype(BF16)
        share_cut(tg_full, (), tg_slot, j)
        text_out[:, at] = text_grad[:texts]
    for j in every:
        shared_cut(tg_full, (), tg_slot, j)
    full = jnp.concatenate([tg_full[0], tg_full[1]], axis=1).astype(F32)
    normed = normed_keep[...]
    mean_grad = jnp.mean(full, axis=-1, keepdims=True)
    mean_cross = jnp.mean(full * normed, axis=-1, keepdims=True)
    dpooled = inv_std * (full - mean_grad - normed * mean_cross)
    dp_out[...] = dpooled.T.astype(BF16).reshape(dp_out.shape)
    spread_z(dp_out, dp_in, 4)

    slab = dp_in.shape[1]
    share = slab // spots
    room = rs_in.shape[1] // 2
    spread_shape = (spots * room, slab)
    row_at = lax.rem(rows_of(spread_shape), room)
    pick = one_hot(
        (row_at < share) & (cols_of(spread_shape) == rows_of(spread_shape) // room * share + row_at)
    ).astype(BF16)
    arrived(dp_in, 4)
    for way, steps in ((0, up_steps), (1, down_steps)):
        for c in range(chunks if steps else 0):
            ring_arrive(way, steps - 1, c)
    joined = jnp.concatenate([dp_in[i] for i in range(planes)], axis=1)
    joined = dot(pick, joined).astype(BF16)
    means = th_all[...].reshape(planes * pad, th_all.shape[2])
    part = dot(joined, means)
    cut = part.shape[1] // 2
    rs_out[...] = jnp.concatenate(
        [part[:, :cut].reshape(spots, room, cut), part[:, cut:].reshape(spots, room, cut)], axis=1
    ).astype(BF16)
    spread_xy(rs_out, rs_in, 5)
    arrived(rs_in, 5)
    total = jnp.sum(rs_in[...].astype(F32), axis=0)
    down_out[:, pl.ds(0, cut)] = total[:share]
    down_out[:, pl.ds(cut, cut)] = total[room : room + share]

    for copy in core_copies + peer_copies:
        copy.wait_send()
    for slot, src in enumerate((a1_out, a2_out, r1_out, r2_out)):
        for j in every:
            left(src, slot, j)
    left(dp_out, 4)
    left(rs_out, 5)
    for way in (0, 1):
        for step, c in ring_plan[way]:
            ring(way, step, c).wait_send()


def finish(node_ref, text_ref, down_ref, node_out, text_out, down_out):
    node_out[...] = node_ref[...]
    text_out[...] = text_ref[...]
    down_out[...] = down_ref[...]


def column_cuts(half):
    first = LANES if half > LANES else half // 2
    return ((0, first), (first, half - first))


def local(
    tokens,
    up_weight,
    down_weight,
    text_owner,
    text_row,
    node_feat,
    local_weight,
    tile_weight,
    tile_peer,
    boundary_rows,
    self_weight,
    neigh_weight,
    node_cot,
    planes,
):
    domains = lax.axis_size("dom")
    spots = domains // planes
    rows, width = tokens.shape
    texts = rows // SEQ
    pad = -(-texts // LANES) * LANES
    nodes, half = node_feat.shape
    bnd = boundary_rows.shape[1]
    hidden = up_weight.shape[1]
    chunk = min(512, hidden)
    chunks = hidden // chunk
    cuts = column_cuts(half)
    core_slots = 1 + LAYERS + (2 * LAYERS + 1) * len(cuts)
    share = width // domains
    room = -(-share // 8) * 8
    slab = width // planes

    owners = text_owner.reshape(-1, LANES)
    text_rows = text_row.reshape(-1, LANES)
    tile = tile_weight.reshape(nodes * TILES, bnd)

    def vm(*shape, dtype=BF16):
        return pltpu.VMEM(shape, dtype)

    dma = pltpu.SemaphoreType.DMA
    scratch = [
        vm(rows, width),
        vm(chunks, width, chunk),
        vm(hidden, width),
        vm(nodes, half),
        vm(nodes, nodes),
        vm(nodes * TILES, bnd),
        vm(LAYERS, width, half),
        vm(LAYERS, width, half),
        vm(nodes, half),
        vm(LAYERS, half, half),
        vm(LAYERS, half, half),
        vm(pad, width, dtype=F32),
        vm(LAYERS, 2, nodes, half),
        vm(LAYERS, 2, nodes, half),
        vm(LAYERS, 2, nodes, half),
        vm(LAYERS, bnd, half),
        vm(LAYERS, SPAN, bnd, half),
        vm(LAYERS, SPAN, bnd, half),
        vm(LAYERS, SPAN, bnd, half),
        vm(planes, 2 * spots, half),
        vm(planes, 2 * spots, half),
        vm(spots, 2 * planes, half),
        vm(spots, 2 * planes, half),
        vm(spots, 2 * planes, half),
        vm(spots, 2 * planes, half),
        vm(planes, 2 * spots, half),
        vm(planes, 2 * spots, half),
        vm(2, pad, half),
        vm(planes, slab, pad),
        vm(planes, slab, pad),
        vm(planes, pad, hidden),
        vm(spots, 2 * room, hidden // 2),
        vm(spots, 2 * room, hidden // 2),
        vm(domains, LANES, dtype=F32),
        vm(pad, width, dtype=F32),
        vm(pad, width, dtype=F32),
        vm(LAYERS, nodes, half, dtype=F32),
        vm(nodes, TILES * bnd),
        vm(TILES * bnd, nodes),
        vm(nodes, nodes),
        vm(bnd, nodes),
        vm(nodes, SPAN * bnd),
        vm(nodes, half, dtype=F32),
        vm(nodes, 2 * domains),
        vm(2 * domains, nodes),
        vm(2 * domains, 2 * domains),
        vm(2 * domains, 2 * domains),
        vm(2 * domains, pad),
        vm(pad, 2 * domains),
        dma((7,)),
        dma((chunks,)),
        dma((chunks,)),
        dma((2, LAYERS)),
        dma((2, LAYERS)),
        dma((core_slots,)),
        dma((core_slots,)),
        dma((LAYERS, SPAN, len(cuts))),
        dma((LAYERS, SPAN, len(cuts))),
        dma((LAYERS, SPAN, len(cuts))),
        dma((LAYERS, SPAN, len(cuts))),
        dma((6, len(cuts))),
        dma((6, len(cuts))),
        dma((2, max(1, planes // 2), chunks)),
        dma((2, max(1, planes // 2), chunks)),
    ]
    vmem = pl.BlockSpec(memory_space=pltpu.VMEM)
    smem = pl.BlockSpec(memory_space=pltpu.SMEM)
    hbm = pl.BlockSpec(memory_space=pl.ANY)
    out_shape = (
        jax.ShapeDtypeStruct((nodes, half), BF16),
        jax.ShapeDtypeStruct((texts, half), F32),
        jax.ShapeDtypeStruct((share, hidden), F32),
    )
    results = pl.pallas_call(
        functools.partial(kernel, planes, texts, cuts),
        out_shape=tuple(pltpu.VMEM(o.shape, o.dtype) for o in out_shape),
        in_specs=[vmem, vmem, vmem, smem] + [hbm] * 9,
        out_specs=(vmem, vmem, vmem),
        scratch_shapes=scratch,
        compiler_params=pltpu.CompilerParams(
            collective_id=0, has_side_effects=True, vmem_limit_bytes=58 * 2**20
        ),
    )(
        owners,
        text_rows,
        boundary_rows,
        tile_peer,
        tokens,
        up_weight,
        down_weight,
        node_feat,
        local_weight,
        tile,
        self_weight,
        neigh_weight,
        node_cot,
    )
    return pl.pallas_call(
        finish,
        out_shape=out_shape,
        in_specs=[vmem] * 3,
        out_specs=(vmem,) * 3,
    )(*[pltpu.with_memory_space_constraint(r, pltpu.VMEM) for r in results])


def solution(mesh):
    in_specs = (
        P("dom", None),
        P(None, "mp"),
        P("mp", None),
        P(),
        P(),
        P("dom", "mp"),
        P("dom", None),
        P("dom", None, None),
        P("dom", None),
        P("dom", None),
        P(None, None, "mp"),
        P(None, None, "mp"),
        P("dom", "mp"),
    )
    out_specs = (P("dom", "mp"), P("dom", "mp"), P("dom", "mp"))
    domains = mesh.shape["dom"]
    planes = 8 if domains >= 128 else 2
    return jax.shard_map(
        functools.partial(local, planes=planes),
        mesh=mesh,
        in_specs=in_specs,
        out_specs=out_specs,
        check_vma=False,
    )
```

```python
import functools
import math

import jax
import jax.numpy as jnp
import numpy as np
from jax import lax
from jax.experimental import pallas as pl
from jax.experimental.pallas import tpu as pltpu
from jax.sharding import PartitionSpec as P

SEQ = 8
TILES = 4
SPAN = 4
LAYERS = 2
LANES = 128
MESH = pl.DeviceIdType.MESH
BF16 = jnp.bfloat16
F32 = jnp.float32
INV_SQRT2 = float(np.sqrt(0.5))
INV_SQRT2PI = float(1.0 / np.sqrt(2.0 * np.pi))


def dot(left, right):
    return lax.dot_general(left, right, (((1,), (0,)), ((), ())), preferred_element_type=F32)


def dot_nt(left, right):
    return lax.dot_general(left, right, (((1,), (1,)), ((), ())), preferred_element_type=F32)


def gelu(x):
    return (0.5 * x) * (1.0 + lax.erf(x * INV_SQRT2))


def gelu_slope(x):
    return 0.5 * (1.0 + lax.erf(x * INV_SQRT2)) + x * (jnp.exp(-0.5 * x * x) * INV_SQRT2PI)


def rows_of(shape):
    return lax.broadcasted_iota(jnp.int32, shape, 0)


def cols_of(shape):
    return lax.broadcasted_iota(jnp.int32, shape, 1)


def one_hot(mask):
    return jnp.where(mask, 1.0, 0.0)


def eye(size):
    return one_hot(rows_of((size, size)) == cols_of((size, size))).astype(BF16)


def kernel(
    planes,
    texts,
    cuts,
    owner_ref,
    row_ref,
    border_ref,
    peer_ref,
    tokens_hbm,
    up_hbm,
    down_hbm,
    feat_hbm,
    near_hbm,
    tile_hbm,
    self_hbm,
    neigh_hbm,
    cot_hbm,
    node_out,
    text_out,
    down_out,
    tokens,
    up,
    down,
    feat,
    near,
    tile,
    self_w,
    neigh_w,
    cot,
    self_x,
    neigh_x,
    pool_x,
    h_full,
    agg_full,
    gz_full,
    edge_out,
    edge_in,
    back_out,
    back_in,
    a1_out,
    a1_in,
    a2_out,
    a2_in,
    r1_out,
    r1_in,
    r2_out,
    r2_in,
    tg_full,
    dp_out,
    dp_in,
    th_all,
    rs_out,
    rs_in,
    owner_keep,
    pool_keep,
    normed_keep,
    slope_keep,
    tile_w,
    tile_t,
    near_t,
    border_t,
    border_m,
    inv_keep,
    place,
    place_t,
    swap_m,
    swap_t,
    send_m,
    send_t,
    load_sem,
    up_sem,
    down_sem,
    wx_send,
    wx_recv,
    mp_send,
    mp_recv,
    edge_send,
    edge_recv,
    back_send,
    back_recv,
    all_send,
    all_recv,
    ring_send,
    ring_recv,
):
    dom = lax.axis_index("dom")
    core = lax.axis_index("mp")
    other = 1 - core
    domains = planes * a2_in.shape[0]
    spots = domains // planes
    z = dom // spots
    xy = lax.rem(dom, spots)
    half = feat.shape[1]
    nodes = feat.shape[0]
    bnd = edge_in.shape[2]
    pad = th_all.shape[1]
    sent_rows = -(-texts // 16) * 16

    loads = [
        pltpu.make_async_copy(src, dst, load_sem.at[i])
        for i, (src, dst) in enumerate(
            [
                (tokens_hbm, tokens),
                (feat_hbm, feat),
                (near_hbm, near),
                (tile_hbm, tile),
                (self_hbm, self_w),
                (neigh_hbm, neigh_w),
                (cot_hbm, cot),
            ]
        )
    ]
    chunks, _, chunk = up.shape
    up_loads = [
        pltpu.make_async_copy(up_hbm.at[:, pl.ds(c * chunk, chunk)], up.at[c], up_sem.at[c])
        for c in range(chunks)
    ]
    down_loads = [
        pltpu.make_async_copy(
            down_hbm.at[pl.ds(c * chunk, chunk), :],
            down.at[pl.ds(c * chunk, chunk), :],
            down_sem.at[c],
        )
        for c in range(chunks)
    ]
    loads[0].start()
    for c in range(chunks):
        up_loads[c].start()
        down_loads[c].start()
    for load in loads[1:]:
        load.start()

    barrier = pltpu.get_barrier_semaphore()

    def greet(device, mp):
        pl.semaphore_signal(barrier, inc=1, device_id=(device, mp), device_id_type=MESH)

    greet(dom, other)
    for i in range(1, planes):
        greet(lax.rem(z + i, planes) * spots + xy, core)
    for i in range(1, spots):
        greet(z * spots + lax.rem(xy + i, spots), core)
    for o in range(1, SPAN + 1):
        greet(lax.rem(dom + o, domains), core)
        greet(lax.rem(dom + domains - o, domains), core)

    up_steps, down_steps = planes // 2, (planes - 1) // 2
    ring_plan = [
        [(step, c) for step in range(steps) for c in range(chunks)] for steps in (up_steps, down_steps)
    ]
    ring_done = [0, 0]

    def ring(way, step, c):
        if way:
            block, to = lax.rem(z + step, planes), lax.rem(z + planes - 1, planes)
        else:
            block, to = lax.rem(z + planes - step, planes), lax.rem(z + 1, planes)
        view = th_all.at[block, pl.ds(0, sent_rows), pl.ds(c * chunk, chunk)]
        return pltpu.make_async_remote_copy(
            view,
            view,
            ring_send.at[way, step, c],
            ring_recv.at[way, step, c],
            device_id=(to * spots + xy, core),
            device_id_type=MESH,
        )

    def ring_arrive(way, step, c):
        if way:
            block = lax.rem(z + step + 1, planes)
        else:
            block = lax.rem(z + 2 * planes - step - 1, planes)
        view = th_all.at[block, pl.ds(0, sent_rows), pl.ds(c * chunk, chunk)]
        pltpu.make_async_copy(view, view, ring_recv.at[way, step, c]).wait()

    def ring_advance(way, count):
        for step, c in ring_plan[way][ring_done[way] : ring_done[way] + count]:
            if step > 0:
                ring_arrive(way, step - 1, c)
            ring(way, step, c).start()
            ring_done[way] += 1

    swaps = []

    def swap_weights():
        for kind, (src, dst) in enumerate([(self_hbm, self_x), (neigh_hbm, neigh_x)]):
            for layer in range(LAYERS):
                copy = pltpu.make_async_remote_copy(
                    src.at[layer, pl.ds(pl.multiple_of(other * half, half), half)],
                    dst.at[layer],
                    wx_send.at[kind, layer],
                    wx_recv.at[kind, layer],
                    device_id=(dom, other),
                    device_id_type=MESH,
                )
                copy.start()
                swaps.append(copy)

    th_all[:, pl.ds(sent_rows, pad - sent_rows), :] = jnp.zeros(
        (planes, pad - sent_rows, th_all.shape[2]), BF16
    )
    rows = tokens.shape[0]
    mean_m = jnp.where(
        lax.shift_right_logical(cols_of((pad, rows)), 3) == rows_of((pad, rows)), 1.0 / SEQ, 0.0
    ).astype(BF16)
    loads[0].wait()
    for c in range(chunks):
        up_loads[c].wait()
        hidden = gelu(dot(tokens[...], up[c])).astype(BF16)
        mean_h = dot(mean_m, hidden).astype(BF16)
        th_all[z, :, pl.ds(c * chunk, chunk)] = mean_h
        down_loads[c].wait()
        partial = dot(mean_h, down[pl.ds(c * chunk, chunk), :])
        if c == 0:
            pool_keep[...] = partial
            pl.semaphore_wait(barrier, planes - 1 + spots - 1 + 2 * SPAN + 1)
            swap_weights()
        else:
            pool_keep[...] += partial
        ring_advance(0, 1)
        ring_advance(1, 1)

    def to_core(src, dst, slot):
        copy = pltpu.make_async_remote_copy(
            src, dst, mp_send.at[slot], mp_recv.at[slot], device_id=(dom, other), device_id_type=MESH
        )
        copy.start()
        return copy

    pool_copy = to_core(pool_keep.at[pl.ds(0, texts)], pool_x.at[pl.ds(0, texts)], 0)
    lines, lanes = owner_ref.shape
    line_of = rows_of((domains, lines)) * texts // lanes
    low = one_hot(cols_of((domains, lines)) == line_of).astype(BF16)
    high = one_hot(cols_of((domains, lines)) == line_of + 1).astype(BF16)
    shard = (domains, lanes)
    inside = cols_of(shard) + lax.rem(rows_of(shard) * texts, lanes) < lanes

    def by_shard(ref):
        flat = ref[...].astype(F32).astype(BF16)
        turned = [dot(m, flat) for m in (low, high)]
        for bit in range(lanes.bit_length() - 1):
            shift = (lanes - texts) * 2**bit % lanes
            if shift:
                moved = lax.rem(rows_of(shard) // 2**bit, 2) == 1
                turned = [jnp.where(moved, pltpu.roll(m, shift, 1), m) for m in turned]
        return jnp.where(cols_of(shard) < texts, jnp.where(inside, *turned), -1.0)

    owner_of = by_shard(owner_ref)
    row_of = by_shard(row_ref)
    owner_keep[...] = owner_of

    upper = one_hot(rows_of((pad, pad)) < cols_of((pad, pad))).astype(BF16)
    mine = owner_keep[pl.ds(dom, 1), :]
    named = one_hot(rows_of((domains, pad)).astype(F32) == mine)
    earlier = dot(named.astype(BF16), upper)
    first = jnp.where(earlier < 0.5, named, 0.0).reshape(planes, spots, pad)
    second = jnp.where(earlier > 0.5, named, 0.0).reshape(planes, spots, pad)
    send_m[...] = jnp.concatenate([first, second], axis=1).reshape(2 * domains, pad).astype(BF16)
    token_mean = dot(mean_m, tokens[...])

    pool_copy.wait_recv()
    in_text = rows_of((pad, 1)) < texts
    pooled = token_mean + pool_keep[...] + jnp.where(in_text, pool_x[...], 0.0)
    centre = pooled - jnp.mean(pooled, axis=-1, keepdims=True)
    inv_std = lax.rsqrt(jnp.mean(centre * centre, axis=-1, keepdims=True) + 1e-05)
    normed = centre * inv_std
    normed_keep[...] = normed
    own = jnp.where(core == 0, normed[:, :half], normed[:, half:]).astype(BF16)
    a1_out[...] = dot(send_m[...], own).astype(BF16).reshape(a1_out.shape)

    def part_of(ref, index, j):
        if j is None:
            return ref.at[index]
        return ref.at[index, :, pl.ds(*cuts[j])]

    def spread(src, dst, slot, j, count, me, device):
        sems = slot, j or 0
        for i in range(1, count):
            to = lax.rem(me + i, count)
            pltpu.make_async_remote_copy(
                part_of(src, to, j),
                part_of(dst, me, j),
                all_send.at[sems],
                all_recv.at[sems],
                device_id=(device(to), core),
                device_id_type=MESH,
            ).start()
        pltpu.make_async_copy(part_of(src, me, j), part_of(dst, me, j), all_recv.at[sems]).start()

    def spread_z(src, dst, slot, j=None):
        spread(src, dst, slot, j, planes, z, lambda to: to * spots + xy)

    def spread_xy(src, dst, slot, j=None):
        spread(src, dst, slot, j, spots, xy, lambda to: z * spots + to)

    def arrived(dst, slot, j=None):
        part = part_of(dst, pl.ds(0, dst.shape[0]), j)
        pltpu.make_async_copy(part, part, all_recv.at[slot, j or 0]).wait()

    def left(src, slot, j=None):
        part = part_of(src, pl.ds(0, src.shape[0] - 1), j)
        pltpu.make_async_copy(part, part, all_send.at[slot, j or 0]).wait()

    every = range(len(cuts))
    for j in every:
        spread_z(a1_out, a1_in, 0, j)

    mask = owner_of == dom.astype(F32)
    before = dot(one_hot(mask).astype(BF16), upper)
    row0 = jnp.max(jnp.where(mask & (before < 0.5), row_of, -1.0), axis=1, keepdims=True)
    row1 = jnp.max(jnp.where(mask & (before > 0.5), row_of, -1.0), axis=1, keepdims=True)
    node = cols_of((domains, nodes)).astype(F32)
    at0 = one_hot(node == row0).reshape(planes, spots, nodes)
    at1 = one_hot(node == row1).reshape(planes, spots, nodes)
    square = (2 * domains, 2 * domains)

    def swapped(index, inner, outer):
        low = lax.rem(index, inner)
        slot = lax.rem(index // inner, 2)
        high = index // (2 * inner)
        return low * (2 * outer) + slot * outer + high

    swap_m[...] = one_hot(cols_of(square) == swapped(rows_of(square), planes, spots)).astype(BF16)
    swap_t[...] = one_hot(cols_of(square) == swapped(rows_of(square), spots, planes)).astype(BF16)
    at = jnp.concatenate([at0, at1], axis=1).reshape(2 * domains, nodes).astype(BF16)
    place_t[...] = dot(swap_m[...], at).astype(BF16)
    place[...] = dot_nt(eye(nodes), place_t[...]).astype(BF16)
    send_t[...] = dot_nt(eye(pad), send_m[...]).astype(BF16)

    def rows_at(ref, j):
        return ref[:, :, pl.ds(*cuts[j])].reshape(-1, cuts[j][1])

    for j in every:
        arrived(a1_in, 0, j)
        moved = dot(swap_m[...], rows_at(a1_in, j)).astype(BF16)
        a2_out[:, :, pl.ds(*cuts[j])] = moved.reshape(spots, 2 * planes, -1)
        spread_xy(a2_out, a2_in, 1, j)
    ring_advance(0, 1)
    ring_advance(1, 1)

    for load in loads[1:]:
        load.wait()
    tall = tile.shape[0]
    for t in range(TILES):
        pick = one_hot(cols_of((nodes, tall)) == rows_of((nodes, tall)) * TILES + t).astype(BF16)
        tile_w[:, pl.ds(t * bnd, bnd)] = dot(pick, tile[...]).astype(BF16)
    for t in range(TILES):
        tile_t[pl.ds(t * bnd, bnd), :] = dot_nt(
            eye(bnd), tile_w[:, pl.ds(t * bnd, bnd)]
        ).astype(BF16)
    near_t[...] = dot_nt(eye(nodes), near[...]).astype(BF16)
    border = one_hot(rows_of((nodes, bnd)) == border_ref[...]).astype(BF16)
    for o in range(SPAN):
        border_m[:, pl.ds(o * bnd, bnd)] = border
    border_t[...] = dot_nt(eye(bnd), border).astype(BF16)
    degree = (
        1.0
        + dot(near[...], jnp.ones((nodes, half), BF16))
        + dot(tile_w[...], jnp.ones((TILES * bnd, half), BF16))
    )
    inv_keep[...] = 1.0 / degree

    own_k = pl.ds(pl.multiple_of(core * half, half), half)
    other_k = pl.ds(pl.multiple_of(other * half, half), half)

    def rows_in(which, j):
        start, size = cuts[j]
        return pl.ds(pl.multiple_of(which * half + start, math.gcd(half, start, size)), size)

    agg_slot = 1 + LAYERS
    gz_slot = agg_slot + LAYERS * len(cuts)
    tg_slot = gz_slot + LAYERS * len(cuts)
    core_copies, peer_copies = [pool_copy], []

    def share_cut(ref, index, slot, j):
        view = ref.at[(*index, core, slice(None), pl.ds(*cuts[j]))]
        core_copies.append(to_core(view, view, slot + j))

    def shared_cut(ref, index, slot, j):
        view = ref.at[(*index, other, slice(None), pl.ds(*cuts[j]))]
        pltpu.make_async_copy(view, view, mp_recv.at[slot + j]).wait()

    def to_partition(src, dst, send, recv, by):
        copy = pltpu.make_async_remote_copy(
            src,
            dst,
            send,
            recv,
            device_id=(lax.rem(dom + domains + by, domains), core),
            device_id_type=MESH,
        )
        copy.start()
        peer_copies.append(copy)
        return copy

    edge_copies = {}

    def emit_state(layer, j, state):
        at = pl.ds(*cuts[j])
        h_full[layer, core, :, at] = state
        edge_out[layer, :, at] = dot(border_t[...], state).astype(BF16)
        edge_copies[layer, j] = [
            to_partition(
                edge_out.at[layer, :, at],
                edge_in.at[layer, o, :, at],
                edge_send.at[layer, o, j],
                edge_recv.at[layer, o, j],
                o + 1,
            )
            for o in range(SPAN)
        ]

    def emit_gz(layer, j, grad):
        at = pl.ds(*cuts[j])
        gz_full[layer, core, :, at] = (grad * slope_keep[layer, :, at]).astype(BF16)
        share_cut(gz_full, (layer,), gz_slot + layer * len(cuts), j)

    for j in every:
        arrived(a2_in, 1, j)
        start = feat[:, pl.ds(*cuts[j])].astype(F32) + dot(place[...], rows_at(a2_in, j))
        emit_state(0, j, start.astype(BF16))

    for layer in range(LAYERS):
        own_h = h_full.at[layer, core]
        core_copies.append(to_core(own_h, own_h, 1 + layer))
        state = h_full[layer, core]
        total = state.astype(F32) + dot(near[...], state)
        pre = dot(state, self_w[layer, own_k, :])
        other_h = h_full.at[layer, other]
        pltpu.make_async_copy(other_h, other_h, mp_recv.at[1 + layer]).wait()
        pre += dot(h_full[layer, other], self_w[layer, other_k, :])
        ring_advance(1, 3)
        for j in every:
            at = pl.ds(*cuts[j])
            for copy in edge_copies[layer, j]:
                copy.wait_recv()
            here = total[:, cuts[j][0] : sum(cuts[j])]
            for t in range(TILES):
                picked = edge_in[layer, 0, :, at]
                for o in range(1, SPAN):
                    picked = jnp.where(peer_ref[0, t] == o, edge_in[layer, o, :, at], picked)
                here += dot(tile_w[:, pl.ds(t * bnd, bnd)], picked)
            agg = (here * inv_keep[:, at]).astype(BF16)
            agg_full[layer, core, :, at] = agg
            share_cut(agg_full, (layer,), agg_slot + layer * len(cuts), j)
            pre += dot(agg, neigh_w[layer, rows_in(core, j), :])
        for j in every:
            shared_cut(agg_full, (layer,), agg_slot + layer * len(cuts), j)
            if j < len(cuts) - 1:
                pre += dot(agg_full[layer, other, :, pl.ds(*cuts[j])], neigh_w[layer, rows_in(other, j), :])
        last = agg_full[layer, other, :, pl.ds(*cuts[-1])]
        kept = []
        for j in every:
            at = pl.ds(*cuts[j])
            done = pre[:, cuts[j][0] : sum(cuts[j])] + dot(
                last, neigh_w[layer, rows_in(other, len(cuts) - 1), at]
            )
            if layer < LAYERS - 1:
                emit_state(layer + 1, j, gelu(done).astype(BF16))
            else:
                slope_keep[layer, :, at] = gelu_slope(done)
                emit_gz(layer, j, cot[:, at].astype(F32))
            kept.append(done)
        for j in every:
            at = pl.ds(*cuts[j])
            if layer < LAYERS - 1:
                slope_keep[layer, :, at] = gelu_slope(kept[j])
            else:
                node_out[:, at] = gelu(kept[j]).astype(BF16)

    for copy in swaps:
        copy.wait()
    for layer in reversed(range(LAYERS)):
        gz = gz_full[layer, core]
        self_part = dot_nt(gz, self_w[layer, own_k, :])
        mean_part = dot_nt(gz, neigh_w[layer, own_k, :])
        for j in every:
            shared_cut(gz_full, (layer,), gz_slot + layer * len(cuts), j)
        gz = gz_full[layer, other]
        back_copies, scaled = [], []
        for j in every:
            at = pl.ds(*cuts[j])
            mean = mean_part[:, cuts[j][0] : sum(cuts[j])] + dot_nt(gz, neigh_x[layer, at, :])
            scaled.append((mean * inv_keep[:, at]).astype(BF16))
            pieces = [dot(tile_t[pl.ds(t * bnd, bnd), :], scaled[j]) for t in range(TILES)]
            sent = []
            for o in range(SPAN):
                bundle = jnp.where(peer_ref[0, 0] == o, pieces[0], 0.0)
                for t in range(1, TILES):
                    bundle += jnp.where(peer_ref[0, t] == o, pieces[t], 0.0)
                back_out[layer, o, :, at] = bundle.astype(BF16)
                sent.append(
                    to_partition(
                        back_out.at[layer, o, :, at],
                        back_in.at[layer, o, :, at],
                        back_send.at[layer, o, j],
                        back_recv.at[layer, o, j],
                        -(o + 1),
                    )
                )
            back_copies.append(sent)
        self_part += dot_nt(gz, self_x[layer])
        grads = [
            self_part[:, cuts[j][0] : sum(cuts[j])]
            + scaled[j].astype(F32)
            + dot(near_t[...], scaled[j])
            for j in every
        ]
        ring_advance(0, 4)
        for j in every:
            at = pl.ds(*cuts[j])
            for copy in back_copies[j]:
                copy.wait_recv()
            grad = grads[j] + dot(
                border_m[...], back_in[layer, :, :, at].reshape(SPAN * bnd, cuts[j][1])
            )
            if layer > 0:
                emit_gz(layer - 1, j, grad)
            else:
                back = dot(place_t[...], grad.astype(BF16)).astype(BF16)
                r1_out[:, :, at] = back.reshape(spots, 2 * planes, -1)
                spread_xy(r1_out, r1_in, 2, j)

    ring_advance(0, len(ring_plan[0]))
    ring_advance(1, len(ring_plan[1]))
    for j in every:
        arrived(r1_in, 2, j)
        moved = dot(swap_t[...], rows_at(r1_in, j)).astype(BF16)
        r2_out[:, :, pl.ds(*cuts[j])] = moved.reshape(planes, 2 * spots, -1)
        spread_z(r2_out, r2_in, 3, j)
    for j in every:
        at = pl.ds(*cuts[j])
        arrived(r2_in, 3, j)
        text_grad = dot(send_t[...], rows_at(r2_in, j))
        tg_full[core, :, at] = text_grad.astype(BF16)
        share_cut(tg_full, (), tg_slot, j)
        text_out[:, at] = text_grad[:texts]
    for j in every:
        shared_cut(tg_full, (), tg_slot, j)
    full = jnp.concatenate([tg_full[0], tg_full[1]], axis=1).astype(F32)
    normed = normed_keep[...]
    mean_grad = jnp.mean(full, axis=-1, keepdims=True)
    mean_cross = jnp.mean(full * normed, axis=-1, keepdims=True)
    dpooled = inv_std * (full - mean_grad - normed * mean_cross)
    dp_out[...] = dpooled.T.astype(BF16).reshape(dp_out.shape)
    spread_z(dp_out, dp_in, 4)

    slab = dp_in.shape[1]
    share = slab // spots
    room = rs_in.shape[1] // 2
    spread_shape = (spots * room, slab)
    row_at = lax.rem(rows_of(spread_shape), room)
    pick = one_hot(
        (row_at < share) & (cols_of(spread_shape) == rows_of(spread_shape) // room * share + row_at)
    ).astype(BF16)
    arrived(dp_in, 4)
    for way, steps in ((0, up_steps), (1, down_steps)):
        for c in range(chunks if steps else 0):
            ring_arrive(way, steps - 1, c)
    joined = jnp.concatenate([dp_in[i] for i in range(planes)], axis=1)
    joined = dot(pick, joined).astype(BF16)
    means = th_all[...].reshape(planes * pad, th_all.shape[2])
    part = dot(joined, means)
    cut = part.shape[1] // 2
    rs_out[...] = jnp.concatenate(
        [part[:, :cut].reshape(spots, room, cut), part[:, cut:].reshape(spots, room, cut)], axis=1
    ).astype(BF16)
    spread_xy(rs_out, rs_in, 5)
    arrived(rs_in, 5)
    total = jnp.sum(rs_in[...].astype(F32), axis=0)
    down_out[:, pl.ds(0, cut)] = total[:share]
    down_out[:, pl.ds(cut, cut)] = total[room : room + share]

    for copy in core_copies + peer_copies:
        copy.wait_send()
    for slot, src in enumerate((a1_out, a2_out, r1_out, r2_out)):
        for j in every:
            left(src, slot, j)
    left(dp_out, 4)
    left(rs_out, 5)
    for way in (0, 1):
        for step, c in ring_plan[way]:
            ring(way, step, c).wait_send()


def finish(node_ref, text_ref, down_ref, node_out, text_out, down_out):
    node_out[...] = node_ref[...]
    text_out[...] = text_ref[...]
    down_out[...] = down_ref[...]


def column_cuts(half):
    first = LANES if half > LANES else half // 2
    return ((0, first), (first, half - first))


def local(
    tokens,
    up_weight,
    down_weight,
    text_owner,
    text_row,
    node_feat,
    local_weight,
    tile_weight,
    tile_peer,
    boundary_rows,
    self_weight,
    neigh_weight,
    node_cot,
    planes,
):
    domains = lax.axis_size("dom")
    spots = domains // planes
    rows, width = tokens.shape
    texts = rows // SEQ
    pad = -(-texts // LANES) * LANES
    nodes, half = node_feat.shape
    bnd = boundary_rows.shape[1]
    hidden = up_weight.shape[1]
    chunk = min(512, hidden)
    chunks = hidden // chunk
    cuts = column_cuts(half)
    core_slots = 1 + LAYERS + (2 * LAYERS + 1) * len(cuts)
    share = width // domains
    room = -(-share // 8) * 8
    slab = width // planes

    owners = text_owner.reshape(-1, LANES)
    text_rows = text_row.reshape(-1, LANES)
    tile = tile_weight.reshape(nodes * TILES, bnd)

    def vm(*shape, dtype=BF16):
        return pltpu.VMEM(shape, dtype)

    dma = pltpu.SemaphoreType.DMA
    scratch = [
        vm(rows, width),
        vm(chunks, width, chunk),
        vm(hidden, width),
        vm(nodes, half),
        vm(nodes, nodes),
        vm(nodes * TILES, bnd),
        vm(LAYERS, width, half),
        vm(LAYERS, width, half),
        vm(nodes, half),
        vm(LAYERS, half, half),
        vm(LAYERS, half, half),
        vm(pad, width, dtype=F32),
        vm(LAYERS, 2, nodes, half),
        vm(LAYERS, 2, nodes, half),
        vm(LAYERS, 2, nodes, half),
        vm(LAYERS, bnd, half),
        vm(LAYERS, SPAN, bnd, half),
        vm(LAYERS, SPAN, bnd, half),
        vm(LAYERS, SPAN, bnd, half),
        vm(planes, 2 * spots, half),
        vm(planes, 2 * spots, half),
        vm(spots, 2 * planes, half),
        vm(spots, 2 * planes, half),
        vm(spots, 2 * planes, half),
        vm(spots, 2 * planes, half),
        vm(planes, 2 * spots, half),
        vm(planes, 2 * spots, half),
        vm(2, pad, half),
        vm(planes, slab, pad),
        vm(planes, slab, pad),
        vm(planes, pad, hidden),
        vm(spots, 2 * room, hidden // 2),
        vm(spots, 2 * room, hidden // 2),
        vm(domains, LANES, dtype=F32),
        vm(pad, width, dtype=F32),
        vm(pad, width, dtype=F32),
        vm(LAYERS, nodes, half, dtype=F32),
        vm(nodes, TILES * bnd),
        vm(TILES * bnd, nodes),
        vm(nodes, nodes),
        vm(bnd, nodes),
        vm(nodes, SPAN * bnd),
        vm(nodes, half, dtype=F32),
        vm(nodes, 2 * domains),
        vm(2 * domains, nodes),
        vm(2 * domains, 2 * domains),
        vm(2 * domains, 2 * domains),
        vm(2 * domains, pad),
        vm(pad, 2 * domains),
        dma((7,)),
        dma((chunks,)),
        dma((chunks,)),
        dma((2, LAYERS)),
        dma((2, LAYERS)),
        dma((core_slots,)),
        dma((core_slots,)),
        dma((LAYERS, SPAN, len(cuts))),
        dma((LAYERS, SPAN, len(cuts))),
        dma((LAYERS, SPAN, len(cuts))),
        dma((LAYERS, SPAN, len(cuts))),
        dma((6, len(cuts))),
        dma((6, len(cuts))),
        dma((2, max(1, planes // 2), chunks)),
        dma((2, max(1, planes // 2), chunks)),
    ]
    vmem = pl.BlockSpec(memory_space=pltpu.VMEM)
    smem = pl.BlockSpec(memory_space=pltpu.SMEM)
    hbm = pl.BlockSpec(memory_space=pl.ANY)
    out_shape = (
        jax.ShapeDtypeStruct((nodes, half), BF16),
        jax.ShapeDtypeStruct((texts, half), F32),
        jax.ShapeDtypeStruct((share, hidden), F32),
    )
    results = pl.pallas_call(
        functools.partial(kernel, planes, texts, cuts),
        out_shape=tuple(pltpu.VMEM(o.shape, o.dtype) for o in out_shape),
        in_specs=[vmem, vmem, vmem, smem] + [hbm] * 9,
        out_specs=(vmem, vmem, vmem),
        scratch_shapes=scratch,
        compiler_params=pltpu.CompilerParams(
            collective_id=0, has_side_effects=True, vmem_limit_bytes=58 * 2**20
        ),
    )(
        owners,
        text_rows,
        boundary_rows,
        tile_peer,
        tokens,
        up_weight,
        down_weight,
        node_feat,
        local_weight,
        tile,
        self_weight,
        neigh_weight,
        node_cot,
    )
    return pl.pallas_call(
        finish,
        out_shape=out_shape,
        in_specs=[vmem] * 3,
        out_specs=(vmem,) * 3,
    )(*[pltpu.with_memory_space_constraint(r, pltpu.VMEM) for r in results])


def solution(mesh):
    in_specs = (
        P("dom", None),
        P(None, "mp"),
        P("mp", None),
        P(),
        P(),
        P("dom", "mp"),
        P("dom", None),
        P("dom", None, None),
        P("dom", None),
        P("dom", None),
        P(None, None, "mp"),
        P(None, None, "mp"),
        P("dom", "mp"),
    )
    out_specs = (P("dom", "mp"), P("dom", "mp"), P("dom", "mp"))
    domains = mesh.shape["dom"]
    planes = 8 if domains >= 128 else 2
    return jax.shard_map(
        functools.partial(local, planes=planes),
        mesh=mesh,
        in_specs=in_specs,
        out_specs=out_specs,
        check_vma=False,
    )
```
